128 devices in a mesh: ctx: 16 (over y_lo, z, core), head: 8 (over x, y_hi).
Axes of the slice: x: 4, y: 4 (y_hi: 2, y_lo: 2; y = y_hi * 2 + y_lo), z: 4, core: 2. Of those that a mesh axis runs over, the one named last changes fastest.
Arguments:
- queries: bfloat16 [2048, 36864], P('ctx', 'head'), may hold values from -296 to 296
- latent_keys: bfloat16 [2048, 576], P('ctx'), may hold values from -9 to 9
- block_order: int32 [16], replicated, may hold values from 0 to 15, each once
- out_grad: bfloat16 [2048, 32768], P('ctx', 'head'), may hold values from -6 to 6
Outputs:
- attended: bfloat16 [2048, 32768], P('ctx', 'head')
- query_grad: bfloat16 [2048, 36864], P('ctx', 'head')
- latent_grad: bfloat16 [2048, 576], P('ctx')
The draws below stay inside these ranges and needn't reach their ends.
Inputs may be any that keep to these rules, and one draw needn't show every extreme that they name: `block_order`: a permutation: each block index once.
All inputs are finite; a program needn't handle non-finite values.
Results may differ from the reference program's by a relative error of at most 0.034.
Values may be sent and summed in bfloat16 or wider, within the bound.
A program may use at most 64 MiB of HBM per device.

```python
import jax
import jax.numpy as jnp
from jax import lax

TOK_DEV = 128
HEADS = 64
LATENT = 512
ROPE = 64
LEN = 2048
BLOCKS = 16


def shared_latent(key):
    base = jnp.clip(jax.random.normal(key, (LEN, LATENT + ROPE), jnp.float32), -4.0, 4.0)
    return base


def draw_latent_keys(key, part):
    base = shared_latent(key)
    return base.astype(jnp.bfloat16)


def draw_queries(key, part):
    key = jax.random.fold_in(key, 5)
    first = jax.random.fold_in(key, 0)
    values = jnp.clip(jax.random.normal(first, (LEN, HEADS, LATENT + ROPE), jnp.float32), -4.0, 4.0)
    return values.reshape(LEN, HEADS * (LATENT + ROPE)).astype(jnp.bfloat16)


def steps_of(rng, dims, shards, least, largest):
    factor_of = 1.0
    for axis_at, shards_of in shards:
        steps = jax.random.uniform(jax.random.fold_in(jax.random.fold_in(rng, 6), axis_at), (shards_of,), jnp.float32, least / len(shards), largest / len(shards))
        factor_of = factor_of * jnp.repeat(jnp.exp(steps), dims[axis_at] // shards_of).reshape((-1,) + (1,) * (len(dims) - 1 - axis_at))
    return factor_of


def scatter_about(own_key, dims, width, most, cuts=(), kind=jnp.bfloat16):
    factor_of = steps_of(own_key, dims, cuts, -0.22, 0.18) if cuts else 1.0
    drawn = jax.random.normal(own_key, dims, jnp.float32) * width * factor_of
    return jnp.minimum(jnp.maximum(drawn, -most), most).astype(kind)


def setup_inputs(seed: int = 0) -> dict:
    arg_keys = jax.random.split(jax.random.key(seed), 5)
    return {
        "queries": draw_queries(jax.random.fold_in(arg_keys[4], 71), 0),
        "latent_keys": draw_latent_keys(jax.random.fold_in(arg_keys[4], 71), 0),
        "block_order": jax.random.permutation(arg_keys[2], BLOCKS).astype(jnp.int32),
        "out_grad": scatter_about(arg_keys[3], (LEN, HEADS * LATENT), 1.0, 6.0, ((0, 16), (1, 8))),
    }


score_scale = 192.0 ** -0.5
masked_value = -1.0e30


def reference(queries, latent_keys, block_order, out_grad):
    kdim = LATENT + ROPE
    rows = jnp.arange(LEN, dtype=jnp.int32)
    position = block_order[rows // TOK_DEV] * TOK_DEV + rows % TOK_DEV
    visible = position[None, :] <= position[:, None]
    query_heads = queries.reshape(LEN, HEADS, kdim).transpose(1, 0, 2)
    grad_heads = out_grad.reshape(LEN, HEADS, LATENT).transpose(1, 0, 2)
    values = latent_keys[:, :LATENT]

    def one_head(key_total, pair):
        query_one, grad_one = pair
        score = jnp.dot(query_one, latent_keys.T, preferred_element_type=jnp.float32) * score_scale
        score = jnp.where(visible, score, masked_value)
        top = jnp.max(score, axis=1, keepdims=True)
        lse = top + jnp.log(jnp.sum(jnp.exp(score - top), axis=1, keepdims=True))
        prob = jnp.where(visible, jnp.exp(score - lse), 0.0)
        prob_b = prob.astype(jnp.bfloat16)
        attended = jnp.dot(prob_b, values, preferred_element_type=jnp.float32).astype(jnp.bfloat16)
        delta = jnp.sum(attended.astype(jnp.float32) * grad_one.astype(jnp.float32), axis=1, keepdims=True)
        dprob = jnp.dot(grad_one, values.T, preferred_element_type=jnp.float32)
        dscore = (prob * (dprob - delta)).astype(jnp.bfloat16)
        query_grad = (score_scale * jnp.dot(dscore, latent_keys, preferred_element_type=jnp.float32)).astype(jnp.bfloat16)
        key_part = score_scale * jnp.dot(dscore.T, query_one, preferred_element_type=jnp.float32)
        value_part = jnp.dot(prob_b.T, grad_one, preferred_element_type=jnp.float32)
        key_total = key_total + key_part + jnp.pad(value_part, ((0, 0), (0, ROPE)))
        return key_total, (attended, query_grad)

    start_total = jnp.zeros((LEN, kdim), jnp.float32)
    key_total, (outputs, query_grads) = lax.scan(one_head, start_total, (query_heads, grad_heads))
    attended = outputs.transpose(1, 0, 2).reshape(LEN, HEADS * LATENT)
    query_grad = query_grads.transpose(1, 0, 2).reshape(LEN, HEADS * kdim)
    return attended, query_grad, key_total.astype(jnp.bfloat16)
```

```python
import functools

import jax
import jax.numpy as jnp
from jax import lax
from jax.experimental import pallas as pl
from jax.experimental.pallas import tpu as pltpu
from jax.sharding import PartitionSpec as P

HEADS = 8
TOK = 128
LAT = 512
KD = 576
ROWS = HEADS * TOK
CHIPS = 8
KEYS = CHIPS * 2 * TOK
SCALE = 192.0**-0.5
LOG2E = 1.4426950408889634
MASKED = -1.0e30
MESH = pl.DeviceIdType.MESH

HALF = KD // 2
A_PIECE = 80
A_ROWS = 4 * A_PIECE
B_ROWS = KD - A_ROWS
B_PIECE = B_ROWS // 8

NN = (((1,), (0,)), ((), ()))
NT = (((1,), (1,)), ((), ()))

A_ORDER = (0, 1, 3, 4, 2, 5, 7, 6)
B_ORDER = (6, 5, 7, 2, 4, 1, 3, 0)
C_TILE = 256


def back(i):
    return (i // 4) * 4 + (4 - i % 4) % 4


def dot(a, b, dims):
    return lax.dot_general(a, b, dims, preferred_element_type=jnp.float32)


def kernel(
    order_ref, q_hbm, k_hbm, g_hbm,
    at_hbm, qg_hbm, kg_hbm,
    q_in, k_in, g_in, q_s, g_s, q_t, g_t, k_t,
    score, dprob, top, total, weighted, lse, delta, prob_b, dscore,
    mine, csend, crecv, chip, arecv, asum, a2recv, a3, a3recv,
    brecv, bsum, b2recv, b3, b3recv, out_t, at_v, qg_v, kg_v,
    in_sem, out_sem,
    k_send, k_recv, y_send, y_recv, f_send, f_recv,
    c_ssem, c_rsem, a1_ssem, a1_rsem, a2_ssem, a2_rsem, a3_ssem, a3_rsem,
    b1_ssem, b1_rsem, b2_ssem, b2_rsem, b3_ssem, b3_rsem,
):
    f32, bf16 = jnp.float32, jnp.bfloat16
    ctx, head = lax.axis_index("ctx"), lax.axis_index("head")
    core = lax.rem(ctx, 2)
    z = lax.rem(ctx // 2, 4)
    y_lo = ctx // 8
    x, y_hi = head // 2, lax.rem(head, 2)

    def chip_of(i, other=0):
        yy = lax.rem(y_lo + i // 4, 2)
        zz = lax.rem(z + i % 4, 4)
        cc = lax.rem(core + other, 2)
        return (yy * 4 + zz) * 2 + cc

    def on_ctx(i):
        return (chip_of(i), head)

    def head_of(k):
        return lax.rem(x + k // 2, 4) * 2 + lax.rem(y_hi + k % 2, 2)

    def on_head(k):
        return (ctx, head_of(k))

    peer = (chip_of(0, 1), head)

    def y_neighbour(step):
        y = lax.rem(y_hi * 2 + y_lo + step, 4)
        return ((lax.rem(y, 2) * 4 + z) * 2 + core, x * 2 + y // 2)

    y_next = (y_neighbour(1), y_neighbour(3))

    load_k = pltpu.make_async_copy(k_hbm, k_in, in_sem.at[0])
    load_q = pltpu.make_async_copy(q_hbm, q_in, in_sem.at[1])
    load_g = pltpu.make_async_copy(g_hbm, g_in, in_sem.at[2])
    load_k.start()
    load_q.start()
    load_g.start()

    barrier = pltpu.get_barrier_semaphore()
    others = [peer] + [on_ctx(i) for i in range(1, 8)] + [on_head(k) for k in range(1, 8)]
    others += [y_next[0], y_next[1]]
    for other in others:
        pl.semaphore_signal(barrier, inc=1, device_id=other, device_id_type=MESH)

    load_k.wait()
    k_t[:, 0:TOK] = k_in[...].T

    def slot(i, u):
        return pl.ds((2 * i + u) * TOK, TOK)

    def send(src, dst, ssem, rsem, device):
        copy = pltpu.make_async_remote_copy(
            src_ref=src, dst_ref=dst, send_sem=ssem, recv_sem=rsem,
            device_id=device, device_id_type=MESH,
        )
        copy.start()
        return copy

    pl.semaphore_wait(barrier, len(others))

    own = k_t.at[:, slot(0, 0)]
    z_copy, y_copy, f_copy = {}, {}, {}
    f_copy[0] = send(own, k_t.at[:, slot(0, 1)], f_send.at[0], f_recv.at[0], peer)
    for i in (1, 3, 2):
        z_copy[back(i)] = send(own, k_t.at[:, slot(back(i), 0)], k_send.at[back(i)], k_recv.at[back(i)], on_ctx(i))

    def across_y(i):
        for n in range(2):
            rows = pl.ds(n * HALF, HALF)
            y_copy[4 + i, n] = send(
                k_t.at[rows, slot(i, 0)], k_t.at[rows, slot(4 + i, 0)],
                y_send.at[i, n], y_recv.at[i, n], y_next[n],
            )

    across_y(0)

    def hand_on(i):
        if i < 4:
            z_copy[i].wait_recv()
            across_y(i)
        else:
            y_copy[i, 0].wait_recv()
            y_copy[i, 1].wait_recv()
        f_copy[i] = send(k_t.at[:, slot(i, 0)], k_t.at[:, slot(i, 1)], f_send.at[i], f_recv.at[i], peer)

    load_q.wait()
    load_g.wait()
    for h in range(HEADS):
        rows = pl.ds(h * TOK, TOK)
        qh = q_in[:, h * KD : (h + 1) * KD]
        q_s[rows, :] = qh
        q_t[:, rows] = (qh.astype(f32) * SCALE).astype(bf16).T
        gh = g_in[:, h * LAT : (h + 1) * LAT]
        g_s[rows, :] = gh
        g_t[:, rows] = gh.T

    top[...] = jnp.full((ROWS, TOK), MASKED, f32)
    total[...] = jnp.zeros((ROWS, TOK), f32)
    weighted[...] = jnp.zeros((ROWS, TOK), f32)
    ahead = lax.broadcasted_iota(jnp.int32, (TOK, TOK), 1) - lax.broadcasted_iota(jnp.int32, (TOK, TOK), 0)
    my_block = order_ref[ctx]

    def scores(i):
        cols = pl.ds(2 * i * TOK, 2 * TOK)
        keys = k_t[:, cols]
        visible = [ahead <= (my_block - order_ref[chip_of(i, u)]) * TOK for u in range(2)]
        for h in range(HEADS):
            rows = pl.ds(h * TOK, TOK)
            sc = dot(q_s[rows, :], keys, NN) * (SCALE * LOG2E)
            dp = dot(g_s[rows, :], keys[:LAT], NN)
            s0 = jnp.where(visible[0], sc[:, :TOK], MASKED)
            s1 = jnp.where(visible[1], sc[:, TOK:], MASKED)
            score[rows, slot(i, 0)] = s0
            score[rows, slot(i, 1)] = s1
            dprob[rows, cols] = dp
            m0 = top[rows, :]
            m1 = jnp.maximum(m0, jnp.maximum(s0, s1))
            shrink = jnp.exp2(m0 - m1)
            e0, e1 = jnp.exp2(s0 - m1), jnp.exp2(s1 - m1)
            top[rows, :] = m1
            total[rows, :] = total[rows, :] * shrink + (e0 + e1)
            weighted[rows, :] = weighted[rows, :] * shrink + (e0 * dp[:, :TOK] + e1 * dp[:, TOK:])

    f_copy[0].wait_recv()
    scores(0)
    hand_on(4)
    hand_on(1)
    hand_on(3)
    f_copy[4].wait_recv()
    scores(4)
    f_copy[1].wait_recv()
    scores(1)
    f_copy[3].wait_recv()
    scores(3)
    hand_on(2)
    f_copy[2].wait_recv()
    scores(2)
    hand_on(5)
    hand_on(7)
    f_copy[5].wait_recv()
    scores(5)
    f_copy[7].wait_recv()
    scores(7)
    hand_on(6)
    f_copy[6].wait_recv()
    scores(6)

    for h in range(HEADS):
        rows = pl.ds(h * TOK, TOK)
        lane_top = top[rows, :]
        row_top = jnp.max(lane_top, axis=1, keepdims=True)
        weight = jnp.exp2(lane_top - row_top)
        row_total = jnp.sum(total[rows, :] * weight, axis=1, keepdims=True)
        row_weighted = jnp.sum(weighted[rows, :] * weight, axis=1, keepdims=True)
        lse[rows, :] = jnp.broadcast_to(row_top + jnp.log2(row_total), (TOK, TOK))
        delta[rows, :] = jnp.broadcast_to(row_weighted / row_total, (TOK, TOK))

    def weights(i):
        for u in range(2):
            cols = slot(i, u)
            p = jnp.exp2(score[:, cols] - lse[...])
            prob_b[:, cols] = p.astype(bf16)
            dscore[:, cols] = (p * (dprob[:, cols] - delta[...])).astype(bf16)

    c_copy, a1_copy, a2_copy, a3_copy = {}, {}, {}, {}
    b1_copy, b2_copy, b3_copy = {}, {}, {}

    def key_grads(i):
        cols = pl.ds(2 * i * TOK, 2 * TOK)
        from_scores = dot(q_t[...], dscore[:, cols], NN)
        from_values = dot(g_t[...], prob_b[:, cols], NN)
        low = from_scores[:LAT] + from_values
        high = from_scores[LAT:]
        mine[i, :LAT, :] = low[:, :TOK]
        mine[i, LAT:, :] = high[:, :TOK]
        csend[i, :LAT, :] = low[:, TOK:].astype(bf16)
        csend[i, LAT:, :] = high[:, TOK:].astype(bf16)

    def to_core(i):
        c_copy[i] = send(csend.at[i], crecv.at[i], c_ssem.at[i], c_rsem.at[i], peer)

    def piece(xx):
        return pl.ds(pl.multiple_of(xx * A_PIECE, 16), A_PIECE)

    def to_links(i):
        c_copy[i].wait_recv()
        chip[i] = (mine[i] + crecv[i].astype(f32)).astype(bf16)
        for dx in (2, 1, 3):
            a1_copy[i, 4 - dx] = send(
                chip.at[i, piece(lax.rem(x + dx, 4))], arecv.at[i, 4 - dx - 1],
                a1_ssem.at[i, 4 - dx - 1], a1_rsem.at[i, 4 - dx - 1], on_head(2 * dx),
            )
        if i:
            j = back(i)
            b1_copy[j] = send(
                chip.at[i, pl.ds(A_ROWS, B_ROWS)], brecv.at[j - 1],
                b1_ssem.at[j - 1], b1_rsem.at[j - 1], on_ctx(i),
            )

    def sum_x(i):
        for dx in (1, 2, 3):
            a1_copy[i, dx].wait_recv()
        part = chip[i, piece(x), :].astype(f32)
        for n in range(3):
            part = part + arecv[i, n].astype(f32)
        asum[i] = part.astype(bf16)
        if i:
            j = back(i)
            a2_copy[j] = send(asum.at[i], a2recv.at[j - 1], a2_ssem.at[j - 1], a2_rsem.at[j - 1], on_ctx(i))

    def back_head(k):
        return ((4 - k // 2) % 4) * 2 + k % 2

    def b_piece(hh):
        return pl.ds(pl.multiple_of(hh * B_PIECE, 16), B_PIECE)

    HEAD_ORDER = (5, 3, 7, 4, 1, 2, 6)

    def b_ctx():
        part = chip[0, A_ROWS:, :].astype(f32)
        for j in range(1, 8):
            b1_copy[j].wait_recv()
            part = part + brecv[j - 1].astype(f32)
        bsum[...] = part.astype(bf16)
        for k in HEAD_ORDER:
            j = back_head(k)
            b2_copy[j] = send(
                bsum.at[b_piece(head_of(k))], b2recv.at[j - 1],
                b2_ssem.at[j - 1], b2_rsem.at[j - 1], on_head(k),
            )

    def a_ctx():
        part = asum[0].astype(f32)
        for j in range(1, 8):
            a2_copy[j].wait_recv()
            part = part + a2recv[j - 1].astype(f32)
        a3[...] = part.astype(bf16)
        for k in HEAD_ORDER:
            j = back_head(k)
            a3_copy[j] = send(a3, a3recv.at[j - 1], a3_ssem.at[j - 1], a3_rsem.at[j - 1], on_head(k))

    def b_head():
        part = bsum[b_piece(head), :].astype(f32)
        for j in range(1, 8):
            b2_copy[j].wait_recv()
            part = part + b2recv[j - 1].astype(f32)
        b3[...] = part.astype(bf16)
        for k in HEAD_ORDER:
            j = back_head(k)
            b3_copy[j] = send(b3, b3recv.at[j - 1], b3_ssem.at[j - 1], b3_rsem.at[j - 1], on_head(k))

    def finish():
        for j in range(1, 8):
            a3_copy[j].wait_recv()
        for dx in range(4):
            first = a3[...] if dx == 0 else a3recv[2 * dx - 1]
            both = first.astype(f32) + a3recv[2 * dx].astype(f32)
            out_t[piece(lax.rem(x + dx, 4)), :] = both.astype(bf16)
        for j in range(8):
            if j:
                b3_copy[j].wait_recv()
            rows = pl.ds(pl.multiple_of(A_ROWS + head_of(j) * B_PIECE, 16), B_PIECE)
            out_t[rows, :] = b3recv[j - 1] if j else b3[...]
        kg_v[...] = out_t[...].T

    at_copy, qg_copy = [], []

    def row_outputs(r):
        rows = pl.ds(r * C_TILE, C_TILE)
        a = dot(prob_b[rows, :], k_t[:LAT, :], NT)
        b = dot(dscore[rows, :], k_t[...], NT) * SCALE
        n = C_TILE // TOK
        for m in range(n):
            h = r * n + m
            at_v[:, h * LAT : (h + 1) * LAT] = a[m * TOK : (m + 1) * TOK].astype(bf16)
            qg_v[:, h * KD : (h + 1) * KD] = b[m * TOK : (m + 1) * TOK].astype(bf16)
        cols = pl.ds(r * n * LAT, n * LAT)
        at_copy.append(pltpu.make_async_copy(at_v.at[:, cols], at_hbm.at[:, cols], out_sem.at[0, r]))
        at_copy[-1].start()
        cols = pl.ds(r * n * KD, n * KD)
        qg_copy.append(pltpu.make_async_copy(qg_v.at[:, cols], qg_hbm.at[:, cols], out_sem.at[1, r]))
        qg_copy[-1].start()

    weights(B_ORDER[0])
    for n, i in enumerate(B_ORDER):
        if n + 1 < CHIPS:
            weights(B_ORDER[n + 1])
        key_grads(i)
        to_core(i)
        if n >= 1:
            to_links(B_ORDER[n - 1])
        if n >= 5:
            sum_x(B_ORDER[n - 5])
    row_outputs(0)
    to_links(B_ORDER[7])
    sum_x(B_ORDER[3])
    sum_x(B_ORDER[4])
    sum_x(B_ORDER[5])
    row_outputs(1)
    sum_x(B_ORDER[6])
    b_ctx()
    row_outputs(2)
    sum_x(B_ORDER[7])
    a_ctx()
    row_outputs(3)
    b_head()
    finish()
    kg_copy = pltpu.make_async_copy(kg_v, kg_hbm, in_sem.at[0])
    kg_copy.start()

    for group in (z_copy, y_copy, f_copy, c_copy, a1_copy, a2_copy, a3_copy, b1_copy, b2_copy, b3_copy):
        for copy in group.values():
            copy.wait_send()
    for copy in at_copy + qg_copy:
        copy.wait()
    kg_copy.wait()


def local(queries, latent_keys, block_order, out_grad):
    f32, bf16 = jnp.float32, jnp.bfloat16
    vmem, dma = pltpu.VMEM, pltpu.SemaphoreType.DMA
    anywhere = pl.BlockSpec(memory_space=pl.ANY)
    scratch = [
        vmem((TOK, HEADS * KD), bf16), vmem((TOK, KD), bf16), vmem((TOK, HEADS * LAT), bf16),
        vmem((ROWS, KD), bf16), vmem((ROWS, LAT), bf16), vmem((KD, ROWS), bf16), vmem((LAT, ROWS), bf16),
        vmem((KD, KEYS), bf16),
        vmem((ROWS, KEYS), f32), vmem((ROWS, KEYS), f32),
        vmem((ROWS, TOK), f32), vmem((ROWS, TOK), f32), vmem((ROWS, TOK), f32),
        vmem((ROWS, TOK), f32), vmem((ROWS, TOK), f32),
        vmem((ROWS, KEYS), bf16), vmem((ROWS, KEYS), bf16),
        vmem((CHIPS, KD, TOK), f32), vmem((CHIPS, KD, TOK), bf16), vmem((CHIPS, KD, TOK), bf16),
        vmem((CHIPS, KD, TOK), bf16),
        vmem((CHIPS, 3, A_PIECE, TOK), bf16), vmem((CHIPS, A_PIECE, TOK), bf16),
        vmem((7, A_PIECE, TOK), bf16), vmem((A_PIECE, TOK), bf16), vmem((7, A_PIECE, TOK), bf16),
        vmem((7, B_ROWS, TOK), bf16), vmem((B_ROWS, TOK), bf16), vmem((7, B_PIECE, TOK), bf16),
        vmem((B_PIECE, TOK), bf16), vmem((7, B_PIECE, TOK), bf16),
        vmem((KD, TOK), bf16),
        vmem((TOK, HEADS * LAT), bf16), vmem((TOK, HEADS * KD), bf16), vmem((TOK, KD), bf16),
        dma((3,)), dma((2, ROWS // C_TILE)),
        dma((4,)), dma((4,)), dma((4, 2)), dma((4, 2)), dma((8,)), dma((8,)),
        dma((8,)), dma((8,)), dma((8, 3)), dma((8, 3)), dma((7,)), dma((7,)), dma((7,)), dma((7,)),
        dma((7,)), dma((7,)), dma((7,)), dma((7,)), dma((7,)), dma((7,)),
    ]
    return pl.pallas_call(
        kernel,
        out_shape=[
            jax.ShapeDtypeStruct((TOK, HEADS * LAT), bf16),
            jax.ShapeDtypeStruct((TOK, HEADS * KD), bf16),
            jax.ShapeDtypeStruct((TOK, KD), bf16),
        ],
        in_specs=[pl.BlockSpec(memory_space=pltpu.SMEM), anywhere, anywhere, anywhere],
        out_specs=[anywhere, anywhere, anywhere],
        scratch_shapes=scratch,
        compiler_params=pltpu.CompilerParams(
            collective_id=0, has_side_effects=True, vmem_limit_bytes=60 * 2**20
        ),
        cost_estimate=pl.CostEstimate(flops=14 * 10**9, bytes_accessed=5 * 10**6, transcendentals=4 * 10**6),
    )(block_order, queries, latent_keys, out_grad)


def solution(mesh):
    return jax.shard_map(
        local,
        mesh=mesh,
        in_specs=(P("ctx", "head"), P("ctx", None), P(), P("ctx", "head")),
        out_specs=(P("ctx", "head"), P("ctx", "head"), P("ctx", None)),
        check_vma=False,
    )
```

```python
import functools

import jax
import jax.numpy as jnp
from jax import lax
from jax.experimental import pallas as pl
from jax.experimental.pallas import tpu as pltpu
from jax.sharding import PartitionSpec as P

HEADS = 8
TOK = 128
LAT = 512
KD = 576
ROWS = HEADS * TOK
CHIPS = 8
KEYS = CHIPS * 2 * TOK
SCALE = 192.0**-0.5
LOG2E = 1.4426950408889634
MASKED = -1.0e30
MESH = pl.DeviceIdType.MESH
SPLIT = 4

PARTS = 4
PART = KD // PARTS
A_PIECE = 80
A_ROWS = 4 * A_PIECE
B_ROWS = KD - A_ROWS
B_PIECE = B_ROWS // 8

NN = (((1,), (0,)), ((), ()))
NT = (((1,), (1,)), ((), ()))

A_ORDER = (0, 1, 3, 4, 2, 5, 7, 6)
B_ORDER = (6, 5, 7, 2, 4, 1, 3, 0)


def back(i):
    return (i // 4) * 4 + (4 - i % 4) % 4


def dot(a, b, dims):
    return lax.dot_general(a, b, dims, preferred_element_type=jnp.float32)


def kernel(
    order_ref, q_hbm, k_hbm, g_hbm,
    at_hbm, qg_hbm, kg_hbm,
    q_in, g_in, q_s, g_s, q_t, g_t, k_t,
    score, dprob, top, total, weighted, lse, delta, prob_b, dscore,
    mine, csend, crecv, chip, arecv, asum, a2recv, a3, a3recv,
    brecv, bsum, b2recv, b3, b3recv, out_t, at_v, qg_v,
    in_sem, out_sem,
    z_send, z_recv, y_send, y_recv, q_send, q_recv, x_send, x_recv, f_send, f_recv,
    c_ssem, c_rsem, a1_ssem, a1_rsem, a2_ssem, a2_rsem, a3_ssem, a3_rsem,
    b1_ssem, b1_rsem, b2_ssem, b2_rsem, b3_ssem, b3_rsem,
):
    f32, bf16 = jnp.float32, jnp.bfloat16
    ctx, head = lax.axis_index("ctx"), lax.axis_index("head")
    core = lax.rem(ctx, 2)
    z = lax.rem(ctx // 2, 4)
    y_lo = ctx // 8
    x, y_hi = head // 2, lax.rem(head, 2)

    def chip_of(i, other=0):
        yy = lax.rem(y_lo + i // 4, 2)
        zz = lax.rem(z + i % 4, 4)
        cc = lax.rem(core + other, 2)
        return (yy * 4 + zz) * 2 + cc

    def on_ctx(i):
        return (chip_of(i), head)

    def head_of(k):
        return lax.rem(x + k // 2, 4) * 2 + lax.rem(y_hi + k % 2, 2)

    def on_head(k):
        return (ctx, head_of(k))

    peer = (chip_of(0, 1), head)

    def y_neighbour(step):
        y = lax.rem(y_hi * 2 + y_lo + step, 4)
        return ((lax.rem(y, 2) * 4 + z) * 2 + core, x * 2 + y // 2)

    y_next = (y_neighbour(1), y_neighbour(3))

    load_k = pltpu.make_async_copy(k_hbm, k_t.at[0], in_sem.at[0])
    load_q = pltpu.make_async_copy(q_hbm, q_in, in_sem.at[1])
    load_g = pltpu.make_async_copy(g_hbm, g_in, in_sem.at[2])
    load_k.start()
    load_q.start()
    load_g.start()

    barrier = pltpu.get_barrier_semaphore()
    others = [peer, y_next[0], y_next[1]] + [on_ctx(i) for i in (1, 3, 2, 6)] + [on_head(k) for k in (2, 6, 4)]
    for other in others:
        pl.semaphore_signal(barrier, inc=1, device_id=other, device_id_type=MESH)

    def slot(i, u):
        return pl.ds((2 * i + u) * TOK, TOK)

    def keys_at(i, u=0):
        return k_t.at[2 * i + u]

    def send(src, dst, ssem, rsem, device):
        copy = pltpu.make_async_remote_copy(
            src_ref=src, dst_ref=dst, send_sem=ssem, recv_sem=rsem,
            device_id=device, device_id_type=MESH,
        )
        copy.start()
        return copy

    pl.semaphore_wait(barrier, len(others))

    def part_of(j, c):
        return k_t.at[j, pl.ds(c * PART, PART)]

    quarter = pl.ds(pl.multiple_of(x * PART, 16), PART)
    z_copy, y_copy, q_copy, x_copy, f_copy = {}, {}, {}, {}, {}

    def along_z(i, c):
        j = back(i)
        z_copy[j, c] = send(
            k_hbm.at[pl.ds(c * PART, PART)], part_of(2 * j, c), z_send.at[j, c], z_recv.at[j, c], on_ctx(i)
        )

    def across_y(i, c):
        src = part_of(2 * i, c) if i else k_hbm.at[pl.ds(c * PART, PART)]
        y_copy[4 + i, c] = send(src, part_of(2 * (4 + i), c), y_send.at[i, c], y_recv.at[i, c], y_next[c % 2])

    def fetch(i):
        q_copy[i] = send(
            k_hbm.at[quarter], k_t.at[2 * i, quarter], q_send.at[i // 4], q_recv.at[i // 4], on_ctx(i)
        )

    def along_x(i):
        q_copy[i].wait_recv()
        for dx in (2, 1, 3):
            n = 3 - dx
            x_copy[i, n] = send(
                k_t.at[2 * i, quarter], k_t.at[2 * i, quarter],
                x_send.at[i // 4, n], x_recv.at[i // 4, n], on_head(2 * dx),
            )

    def to_other(i):
        src = keys_at(i) if i else k_hbm
        f_copy[i] = send(src, keys_at(i, 1), f_send.at[i], f_recv.at[i], peer)

    def from_z(i, c):
        z_copy[i, c].wait_recv()
        across_y(i, c)

    def from_y(i):
        for c in range(PARTS):
            y_copy[i, c].wait_recv()
        to_other(i)

    def from_x(i):
        for n in range(3):
            x_copy[i, n].wait_recv()
        to_other(i)

    fetch(6)
    fetch(2)
    for c in range(PARTS):
        along_z(1, c)
        along_z(3, c)
        across_y(0, c)
    to_other(0)

    load_q.wait()
    load_g.wait()
    for h in range(HEADS):
        rows = pl.ds(h * TOK, TOK)
        qh = q_in[:, h * KD : (h + 1) * KD]
        q_s[rows, :] = qh
        q_t[:, rows] = (qh.astype(f32) * SCALE).astype(bf16).T
        gh = g_in[:, h * LAT : (h + 1) * LAT]
        g_s[rows, :] = gh
        g_t[:, rows] = gh.T

    top[...] = jnp.full((ROWS, TOK), MASKED, f32)
    total[...] = jnp.zeros((ROWS, TOK), f32)
    weighted[...] = jnp.zeros((ROWS, TOK), f32)
    ahead = lax.broadcasted_iota(jnp.int32, (TOK, TOK), 1) - lax.broadcasted_iota(jnp.int32, (TOK, TOK), 0)
    my_block = order_ref[ctx]

    def scores(i):
        cols = pl.ds(2 * i * TOK, 2 * TOK)
        keys = jnp.concatenate([k_t[2 * i], k_t[2 * i + 1]], axis=1)
        visible = [ahead <= (my_block - order_ref[chip_of(i, u)]) * TOK for u in range(2)]
        for h in range(HEADS):
            rows = pl.ds(h * TOK, TOK)
            sc = dot(q_s[rows, :], keys, NN) * (SCALE * LOG2E)
            dp = dot(g_s[rows, :], keys[:LAT], NN)
            s0 = jnp.where(visible[0], sc[:, :TOK], MASKED)
            s1 = jnp.where(visible[1], sc[:, TOK:], MASKED)
            score[rows, slot(i, 0)] = s0
            score[rows, slot(i, 1)] = s1
            dprob[rows, cols] = dp
            m0 = top[rows, :]
            m1 = jnp.maximum(m0, jnp.maximum(s0, s1))
            shrink = jnp.exp2(m0 - m1)
            e0, e1 = jnp.exp2(s0 - m1), jnp.exp2(s1 - m1)
            top[rows, :] = m1
            total[rows, :] = total[rows, :] * shrink + (e0 + e1)
            weighted[rows, :] = weighted[rows, :] * shrink + (e0 * dp[:, :TOK] + e1 * dp[:, TOK:])

    load_k.wait()
    f_copy[0].wait_recv()
    scores(0)
    along_x(2)
    along_x(6)
    for c in range(PARTS):
        from_z(1, c)
        from_z(3, c)
    to_other(1)
    to_other(3)
    from_y(4)
    for i in (1, 3, 4):
        f_copy[i].wait_recv()
        scores(i)
    from_x(2)
    from_x(6)
    for i in (2, 6):
        f_copy[i].wait_recv()
        scores(i)
    from_y(5)
    from_y(7)
    for i in (5, 7):
        f_copy[i].wait_recv()
        scores(i)

    for h in range(HEADS):
        rows = pl.ds(h * TOK, TOK)
        lane_top = top[rows, :]
        row_top = jnp.max(lane_top, axis=1, keepdims=True)
        weight = jnp.exp2(lane_top - row_top)
        row_total = jnp.sum(total[rows, :] * weight, axis=1, keepdims=True)
        row_weighted = jnp.sum(weighted[rows, :] * weight, axis=1, keepdims=True)
        lse[rows, :] = jnp.broadcast_to(row_top + jnp.log2(row_total), (TOK, TOK))
        delta[rows, :] = jnp.broadcast_to(row_weighted / row_total, (TOK, TOK))

    def weights(i):
        for u in range(2):
            cols = slot(i, u)
            p = jnp.exp2(score[:, cols] - lse[...])
            prob_b[:, cols] = p.astype(bf16)
            dscore[:, cols] = (p * (dprob[:, cols] - delta[...])).astype(bf16)

    c_copy, a1_copy, a2_copy, a3_copy = {}, {}, {}, {}
    b1_copy, b2_copy, b3_copy = {}, {}, {}

    def key_grads(i):
        cols = pl.ds(2 * i * TOK, 2 * TOK)
        from_scores = dot(q_t[...], dscore[:, cols], NN)
        from_values = dot(g_t[...], prob_b[:, cols], NN)
        low = from_scores[:LAT] + from_values
        high = from_scores[LAT:]
        mine[i, :LAT, :] = low[:, :TOK]
        mine[i, LAT:, :] = high[:, :TOK]
        csend[i, :LAT, :] = low[:, TOK:].astype(bf16)
        csend[i, LAT:, :] = high[:, TOK:].astype(bf16)

    def to_core(i):
        c_copy[i] = send(csend.at[i], crecv.at[i], c_ssem.at[i], c_rsem.at[i], peer)

    def piece(xx):
        return pl.ds(pl.multiple_of(xx * A_PIECE, 16), A_PIECE)

    def to_links(i):
        c_copy[i].wait_recv()
        chip[i] = (mine[i] + crecv[i].astype(f32)).astype(bf16)
        for dx in (2, 1, 3):
            a1_copy[i, 4 - dx] = send(
                chip.at[i, piece(lax.rem(x + dx, 4))], arecv.at[i, 4 - dx - 1],
                a1_ssem.at[i, 4 - dx - 1], a1_rsem.at[i, 4 - dx - 1], on_head(2 * dx),
            )
        if i:
            j = back(i)
            b1_copy[j] = send(
                chip.at[i, pl.ds(A_ROWS, B_ROWS)], brecv.at[j - 1],
                b1_ssem.at[j - 1], b1_rsem.at[j - 1], on_ctx(i),
            )

    def sum_x(i):
        for dx in (1, 2, 3):
            a1_copy[i, dx].wait_recv()
        part = chip[i, piece(x), :].astype(f32)
        for n in range(3):
            part = part + arecv[i, n].astype(f32)
        asum[i] = part.astype(bf16)
        if i:
            j = back(i)
            a2_copy[j] = send(asum.at[i], a2recv.at[j - 1], a2_ssem.at[j - 1], a2_rsem.at[j - 1], on_ctx(i))

    def back_head(k):
        return ((4 - k // 2) % 4) * 2 + k % 2

    def b_piece(hh):
        return pl.ds(pl.multiple_of(hh * B_PIECE, 16), B_PIECE)

    HEAD_ORDER = (5, 3, 7, 4, 1, 2, 6)

    def b_ctx():
        part = chip[0, A_ROWS:, :].astype(f32)
        for j in range(1, 8):
            b1_copy[j].wait_recv()
            part = part + brecv[j - 1].astype(f32)
        bsum[...] = part.astype(bf16)
        for k in HEAD_ORDER:
            j = back_head(k)
            b2_copy[j] = send(
                bsum.at[b_piece(head_of(k))], b2recv.at[j - 1],
                b2_ssem.at[j - 1], b2_rsem.at[j - 1], on_head(k),
            )

    def a_ctx():
        part = asum[0].astype(f32)
        for j in range(1, 8):
            a2_copy[j].wait_recv()
            part = part + a2recv[j - 1].astype(f32)
        a3[...] = part.astype(bf16)
        for k in HEAD_ORDER:
            j = back_head(k)
            a3_copy[j] = send(a3, a3recv.at[j - 1], a3_ssem.at[j - 1], a3_rsem.at[j - 1], on_head(k))

    def b_head():
        part = bsum[b_piece(head), :].astype(f32)
        for j in range(1, 8):
            b2_copy[j].wait_recv()
            part = part + b2recv[j - 1].astype(f32)
        b3[...] = part.astype(bf16)
        for k in HEAD_ORDER:
            j = back_head(k)
            b3_copy[j] = send(b3, b3recv.at[j - 1], b3_ssem.at[j - 1], b3_rsem.at[j - 1], on_head(k))

    def finish():
        for j in range(1, 8):
            a3_copy[j].wait_recv()
        for dx in range(4):
            first = a3[...] if dx == 0 else a3recv[2 * dx - 1]
            both = first.astype(f32) + a3recv[2 * dx].astype(f32)
            out_t[piece(lax.rem(x + dx, 4)), :] = both.astype(bf16)
        for j in range(8):
            if j:
                b3_copy[j].wait_recv()
            rows = pl.ds(pl.multiple_of(A_ROWS + head_of(j) * B_PIECE, 16), B_PIECE)
            out_t[rows, :] = b3recv[j - 1] if j else b3[...]

    out_copy = []

    def row_outputs(n):
        if n < 2:
            left, wide, out, first = prob_b, LAT, at_v, n * 256
        else:
            left, wide, out, first = dscore, KD, qg_v, (n - 2) * 256
        size = min(256, wide - first)
        keys = jnp.concatenate([k_t[j, first : first + size, :] for j in range(2 * CHIPS)], axis=1)
        part = dot(left[...], keys, NT)
        if n >= 2:
            part = part * SCALE
        for h in range(HEADS):
            out[:, h * wide + first : h * wide + first + size] = part[h * TOK : (h + 1) * TOK].astype(bf16)
        if n == 1:
            out_copy.append(pltpu.make_async_copy(at_v, at_hbm, out_sem.at[0]))
            out_copy[-1].start()
        if n == 4:
            out_copy.append(pltpu.make_async_copy(qg_v, qg_hbm, out_sem.at[1]))
            out_copy[-1].start()

    groups = [B_ORDER[n : n + 2] for n in range(0, CHIPS, 2)]
    for i in groups[0]:
        weights(i)
    for n, group in enumerate(groups):
        if n + 1 < len(groups):
            for i in groups[n + 1]:
                weights(i)
        for i in group:
            key_grads(i)
        for i in group:
            to_core(i)
        if n >= 1:
            for i in groups[n - 1]:
                to_links(i)
    row_outputs(0)
    for i in groups[3]:
        to_links(i)
    sum_x(B_ORDER[0])
    sum_x(B_ORDER[1])
    sum_x(B_ORDER[2])
    sum_x(B_ORDER[3])
    row_outputs(1)
    row_outputs(2)
    sum_x(B_ORDER[4])
    sum_x(B_ORDER[5])
    sum_x(B_ORDER[6])
    sum_x(B_ORDER[7])
    b_ctx()
    row_outputs(3)
    a_ctx()
    b_head()
    row_outputs(4)
    finish()
    kg_copy = pltpu.make_async_copy(out_t, kg_hbm, in_sem.at[0])
    kg_copy.start()

    for group in (z_copy, y_copy, q_copy, x_copy, f_copy, c_copy, a1_copy, a2_copy, a3_copy, b1_copy, b2_copy, b3_copy):
        for copy in group.values():
            copy.wait_send()
    for copy in out_copy:
        copy.wait()
    kg_copy.wait()


def place(*refs):
    srcs, dsts, held, sems = refs[:3], refs[3:6], refs[6:9], refs[9]
    copies = []
    for n in range(3):
        rows = srcs[n].shape[0] // SPLIT
        for c in range(SPLIT):
            part = pl.ds(c * rows, rows)
            into = pltpu.make_async_copy(srcs[n].at[part], held[n].at[part], sems.at[0, n, c])
            out = pltpu.make_async_copy(held[n].at[part], dsts[n].at[part], sems.at[1, n, c])
            into.start()
            copies.append((into, out))
    for into, out in copies:
        into.wait()
        out.start()
    for into, out in copies:
        out.wait()


def local(queries, latent_keys, block_order, out_grad):
    f32, bf16 = jnp.float32, jnp.bfloat16
    vmem, dma = pltpu.VMEM, pltpu.SemaphoreType.DMA
    anywhere = pl.BlockSpec(memory_space=pl.ANY)
    scratch = [
        vmem((TOK, HEADS * KD), bf16), vmem((TOK, HEADS * LAT), bf16),
        vmem((ROWS, KD), bf16), vmem((ROWS, LAT), bf16), vmem((KD, ROWS), bf16), vmem((LAT, ROWS), bf16),
        vmem((2 * CHIPS, KD, TOK), bf16),
        vmem((ROWS, KEYS), f32), vmem((ROWS, KEYS), f32),
        vmem((ROWS, TOK), f32), vmem((ROWS, TOK), f32), vmem((ROWS, TOK), f32),
        vmem((ROWS, TOK), f32), vmem((ROWS, TOK), f32),
        vmem((ROWS, KEYS), bf16), vmem((ROWS, KEYS), bf16),
        vmem((CHIPS, KD, TOK), f32), vmem((CHIPS, KD, TOK), bf16), vmem((CHIPS, KD, TOK), bf16),
        vmem((CHIPS, KD, TOK), bf16),
        vmem((CHIPS, 3, A_PIECE, TOK), bf16), vmem((CHIPS, A_PIECE, TOK), bf16),
        vmem((7, A_PIECE, TOK), bf16), vmem((A_PIECE, TOK), bf16), vmem((7, A_PIECE, TOK), bf16),
        vmem((7, B_ROWS, TOK), bf16), vmem((B_ROWS, TOK), bf16), vmem((7, B_PIECE, TOK), bf16),
        vmem((B_PIECE, TOK), bf16), vmem((7, B_PIECE, TOK), bf16),
        vmem((KD, TOK), bf16),
        vmem((TOK, HEADS * LAT), bf16), vmem((TOK, HEADS * KD), bf16),
        dma((3,)), dma((2,)),
        dma((4, PARTS)), dma((4, PARTS)), dma((4, PARTS)), dma((4, PARTS)), dma((2,)), dma((2,)), dma((2, 3)), dma((2, 3)),
        dma((8,)), dma((8,)),
        dma((8,)), dma((8,)), dma((8, 3)), dma((8, 3)), dma((7,)), dma((7,)), dma((7,)), dma((7,)),
        dma((7,)), dma((7,)), dma((7,)), dma((7,)), dma((7,)), dma((7,)),
    ]
    attended, query_grad, key_grad = pl.pallas_call(
        kernel,
        out_shape=[
            jax.ShapeDtypeStruct((TOK, HEADS * LAT), bf16),
            jax.ShapeDtypeStruct((TOK, HEADS * KD), bf16),
            jax.ShapeDtypeStruct((KD, TOK), bf16),
        ],
        in_specs=[pl.BlockSpec(memory_space=pltpu.SMEM), anywhere, anywhere, anywhere],
        out_specs=[anywhere, anywhere, anywhere],
        scratch_shapes=scratch,
        compiler_params=pltpu.CompilerParams(
            collective_id=0, has_side_effects=True, vmem_limit_bytes=60 * 2**20
        ),
        cost_estimate=pl.CostEstimate(flops=14 * 10**9, bytes_accessed=5 * 10**6, transcendentals=4 * 10**6),
    )(block_order, queries, latent_keys.T, out_grad)
    results = (attended, query_grad, key_grad)
    attended, query_grad, key_grad = pl.pallas_call(
        place,
        out_shape=[jax.ShapeDtypeStruct(r.shape, r.dtype) for r in results],
        in_specs=[anywhere] * 3,
        out_specs=[anywhere] * 3,
        scratch_shapes=[vmem(r.shape, r.dtype) for r in results] + [dma((2, 3, SPLIT))],
    )(*results)
    return attended, query_grad, key_grad.T


def solution(mesh):
    return jax.shard_map(
        local,
        mesh=mesh,
        in_specs=(P("ctx", "head"), P("ctx", None), P(), P("ctx", "head")),
        out_specs=(P("ctx", "head"), P("ctx", "head"), P("ctx", None)),
        check_vma=False,
    )
```

```python
import functools

import jax
import jax.numpy as jnp
from jax import lax
from jax.experimental import pallas as pl
from jax.experimental.pallas import tpu as pltpu
from jax.sharding import PartitionSpec as P

HEADS = 8
TOK = 128
LAT = 512
KD = 576
ROWS = HEADS * TOK
CHIPS = 8
KEYS = CHIPS * 2 * TOK
SCALE = 192.0**-0.5
LOG2E = 1.4426950408889634
MASKED = -1.0e30
MESH = pl.DeviceIdType.MESH
SPLIT = 4

PARTS = 4
PART = KD // PARTS
A_PIECE = 80
A_ROWS = 4 * A_PIECE
B_ROWS = KD - A_ROWS
B_PIECE = B_ROWS // 8

NN = (((1,), (0,)), ((), ()))
NT = (((1,), (1,)), ((), ()))

B_ORDER = (6, 5, 7, 2, 4, 1, 3, 0)


def back(i):
    return (i // 4) * 4 + (4 - i % 4) % 4


def dot(a, b, dims):
    return lax.dot_general(a, b, dims, preferred_element_type=jnp.float32)


def kernel(
    order_ref, q_hbm, k_hbm, g_hbm,
    at_hbm, qg_hbm, kg_hbm,
    q_in, g_in, q_s, g_s, q_t, g_t, k_t,
    score, dprob, top, total, weighted, lse, delta, prob_b, dscore,
    mine, csend, crecv, chip, arecv, asum, a2recv, a3, a3recv,
    brecv, bsum, b2recv, b3, b3recv, out_t, at_v, qg_v,
    in_sem, out_sem,
    z_send, z_recv, y_send, y_recv, q_send, q_recv, x_send, x_recv, f_send, f_recv,
    c_ssem, c_rsem, a1_ssem, a1_rsem, a2_ssem, a2_rsem, a3_ssem, a3_rsem,
    b1_ssem, b1_rsem, b2_ssem, b2_rsem, b3_ssem, b3_rsem,
):
    f32, bf16 = jnp.float32, jnp.bfloat16
    ctx, head = lax.axis_index("ctx"), lax.axis_index("head")
    core = lax.rem(ctx, 2)
    z = lax.rem(ctx // 2, 4)
    y_lo = ctx // 8
    x, y_hi = head // 2, lax.rem(head, 2)

    def chip_of(i, other=0):
        yy = lax.rem(y_lo + i // 4, 2)
        zz = lax.rem(z + i % 4, 4)
        cc = lax.rem(core + other, 2)
        return (yy * 4 + zz) * 2 + cc

    def on_ctx(i):
        return (chip_of(i), head)

    def head_of(k):
        return lax.rem(x + k // 2, 4) * 2 + lax.rem(y_hi + k % 2, 2)

    def on_head(k):
        return (ctx, head_of(k))

    peer = (chip_of(0, 1), head)

    def y_neighbour(step):
        y = lax.rem(y_hi * 2 + y_lo + step, 4)
        return ((lax.rem(y, 2) * 4 + z) * 2 + core, x * 2 + y // 2)

    y_next = (y_neighbour(1), y_neighbour(3))

    load_k = pltpu.make_async_copy(k_hbm, k_t.at[0], in_sem.at[0])
    load_q = pltpu.make_async_copy(q_hbm, q_in, in_sem.at[1])
    load_g = pltpu.make_async_copy(g_hbm, g_in, in_sem.at[2])
    load_k.start()
    load_q.start()
    load_g.start()

    barrier = pltpu.get_barrier_semaphore()
    others = [peer, y_next[0], y_next[1]] + [on_ctx(i) for i in (1, 3, 2, 6)] + [on_head(k) for k in (2, 6, 4)]
    for other in others:
        pl.semaphore_signal(barrier, inc=1, device_id=other, device_id_type=MESH)

    def slot(i, u):
        return pl.ds((2 * i + u) * TOK, TOK)

    def keys_at(i, u=0):
        return k_t.at[2 * i + u]

    def send(src, dst, ssem, rsem, device):
        copy = pltpu.make_async_remote_copy(
            src_ref=src, dst_ref=dst, send_sem=ssem, recv_sem=rsem,
            device_id=device, device_id_type=MESH,
        )
        copy.start()
        return copy

    pl.semaphore_wait(barrier, len(others))

    def part_of(j, c):
        return k_t.at[j, pl.ds(c * PART, PART)]

    quarter = pl.ds(pl.multiple_of(x * PART, 16), PART)
    z_copy, y_copy, q_copy, x_copy, f_copy = {}, {}, {}, {}, {}

    def along_z(i, c):
        j = back(i)
        z_copy[j, c] = send(
            k_hbm.at[pl.ds(c * PART, PART)], part_of(2 * j, c), z_send.at[j, c], z_recv.at[j, c], on_ctx(i)
        )

    def across_y(i, c):
        src = part_of(2 * i, c) if i else k_hbm.at[pl.ds(c * PART, PART)]
        y_copy[4 + i, c] = send(src, part_of(2 * (4 + i), c), y_send.at[i, c], y_recv.at[i, c], y_next[c % 2])

    def fetch(i):
        q_copy[i] = send(
            k_hbm.at[quarter], k_t.at[2 * i, quarter], q_send.at[i // 4], q_recv.at[i // 4], on_ctx(i)
        )

    def along_x(i):
        q_copy[i].wait_recv()
        for dx in (2, 1, 3):
            n = 3 - dx
            x_copy[i, n] = send(
                k_t.at[2 * i, quarter], k_t.at[2 * i, quarter],
                x_send.at[i // 4, n], x_recv.at[i // 4, n], on_head(2 * dx),
            )

    def to_other(i):
        src = keys_at(i) if i else k_hbm
        f_copy[i] = send(src, keys_at(i, 1), f_send.at[i], f_recv.at[i], peer)

    def from_z(i, c):
        z_copy[i, c].wait_recv()
        across_y(i, c)

    def from_y(i):
        for c in range(PARTS):
            y_copy[i, c].wait_recv()
        to_other(i)

    def from_x(i):
        for n in range(3):
            x_copy[i, n].wait_recv()
        to_other(i)

    fetch(6)
    fetch(2)
    for c in range(PARTS):
        along_z(1, c)
        along_z(3, c)
        across_y(0, c)
    to_other(0)

    load_q.wait()
    load_g.wait()
    for h in range(HEADS):
        rows = pl.ds(h * TOK, TOK)
        qh = q_in[:, h * KD : (h + 1) * KD]
        q_s[rows, :] = qh
        q_t[:, rows] = (qh.astype(f32) * SCALE).astype(bf16).T
        gh = g_in[:, h * LAT : (h + 1) * LAT]
        g_s[rows, :] = gh
        g_t[:, rows] = gh.T

    top[...] = jnp.full((ROWS, TOK), MASKED, f32)
    total[...] = jnp.zeros((ROWS, TOK), f32)
    weighted[...] = jnp.zeros((ROWS, TOK), f32)
    ahead = lax.broadcasted_iota(jnp.int32, (TOK, TOK), 1) - lax.broadcasted_iota(jnp.int32, (TOK, TOK), 0)
    my_block = order_ref[ctx]

    def scores(first, second):
        pair = (first, second)
        keys = jnp.concatenate([k_t[2 * i + u] for i, u in pair], axis=1)
        visible = [ahead <= (my_block - order_ref[chip_of(i, u)]) * TOK for i, u in pair]
        for h in range(HEADS):
            rows = pl.ds(h * TOK, TOK)
            sc = dot(q_s[rows, :], keys, NN) * (SCALE * LOG2E)
            dp = dot(g_s[rows, :], keys[:LAT], NN)
            s0 = jnp.where(visible[0], sc[:, :TOK], MASKED)
            s1 = jnp.where(visible[1], sc[:, TOK:], MASKED)
            score[rows, slot(*first)] = s0
            score[rows, slot(*second)] = s1
            dprob[rows, slot(*first)] = dp[:, :TOK]
            dprob[rows, slot(*second)] = dp[:, TOK:]
            m0 = top[rows, :]
            m1 = jnp.maximum(m0, jnp.maximum(s0, s1))
            shrink = jnp.exp2(m0 - m1)
            e0, e1 = jnp.exp2(s0 - m1), jnp.exp2(s1 - m1)
            top[rows, :] = m1
            total[rows, :] = total[rows, :] * shrink + (e0 + e1)
            weighted[rows, :] = weighted[rows, :] * shrink + (e0 * dp[:, :TOK] + e1 * dp[:, TOK:])

    load_k.wait()
    f_copy[0].wait_recv()
    scores((0, 0), (0, 1))
    along_x(2)
    along_x(6)
    for c in range(PARTS):
        from_z(1, c)
        from_z(3, c)
    to_other(1)
    to_other(3)
    scores((1, 0), (3, 0))
    from_y(4)
    f_copy[1].wait_recv()
    f_copy[3].wait_recv()
    scores((1, 1), (3, 1))
    f_copy[4].wait_recv()
    scores((4, 0), (4, 1))
    from_x(2)
    from_x(6)
    scores((2, 0), (6, 0))
    from_y(5)
    from_y(7)
    scores((5, 0), (7, 0))
    f_copy[2].wait_recv()
    f_copy[6].wait_recv()
    scores((2, 1), (6, 1))
    f_copy[5].wait_recv()
    f_copy[7].wait_recv()
    scores((5, 1), (7, 1))

    for h in range(HEADS):
        rows = pl.ds(h * TOK, TOK)
        lane_top = top[rows, :]
        row_top = jnp.max(lane_top, axis=1, keepdims=True)
        weight = jnp.exp2(lane_top - row_top)
        row_total = jnp.sum(total[rows, :] * weight, axis=1, keepdims=True)
        row_weighted = jnp.sum(weighted[rows, :] * weight, axis=1, keepdims=True)
        lse[rows, :] = jnp.broadcast_to(row_top + jnp.log2(row_total), (TOK, TOK))
        delta[rows, :] = jnp.broadcast_to(row_weighted / row_total, (TOK, TOK))

    def weights(i):
        for u in range(2):
            cols = slot(i, u)
            p = jnp.exp2(score[:, cols] - lse[...])
            prob_b[:, cols] = p.astype(bf16)
            dscore[:, cols] = (p * (dprob[:, cols] - delta[...])).astype(bf16)

    c_copy, a1_copy, a2_copy, a3_copy = {}, {}, {}, {}
    b1_copy, b2_copy, b3_copy = {}, {}, {}

    def key_grads(i):
        cols = pl.ds(2 * i * TOK, 2 * TOK)
        from_scores = dot(q_t[...], dscore[:, cols], NN)
        from_values = dot(g_t[...], prob_b[:, cols], NN)
        low = from_scores[:LAT] + from_values
        high = from_scores[LAT:]
        mine[i, :LAT, :] = low[:, :TOK]
        mine[i, LAT:, :] = high[:, :TOK]
        csend[i, :LAT, :] = low[:, TOK:].astype(bf16)
        csend[i, LAT:, :] = high[:, TOK:].astype(bf16)

    def to_core(i):
        c_copy[i] = send(csend.at[i], crecv.at[i], c_ssem.at[i], c_rsem.at[i], peer)

    def piece(xx):
        return pl.ds(pl.multiple_of(xx * A_PIECE, 16), A_PIECE)

    def to_links(i):
        c_copy[i].wait_recv()
        chip[i] = (mine[i] + crecv[i].astype(f32)).astype(bf16)
        for dx in (2, 1, 3):
            a1_copy[i, 4 - dx] = send(
                chip.at[i, piece(lax.rem(x + dx, 4))], arecv.at[i, 4 - dx - 1],
                a1_ssem.at[i, 4 - dx - 1], a1_rsem.at[i, 4 - dx - 1], on_head(2 * dx),
            )
        if i:
            j = back(i)
            b1_copy[j] = send(
                chip.at[i, pl.ds(A_ROWS, B_ROWS)], brecv.at[j - 1],
                b1_ssem.at[j - 1], b1_rsem.at[j - 1], on_ctx(i),
            )

    def sum_x(i):
        for dx in (1, 2, 3):
            a1_copy[i, dx].wait_recv()
        part = chip[i, piece(x), :].astype(f32)
        for n in range(3):
            part = part + arecv[i, n].astype(f32)
        asum[i] = part.astype(bf16)
        if i:
            j = back(i)
            a2_copy[j] = send(asum.at[i], a2recv.at[j - 1], a2_ssem.at[j - 1], a2_rsem.at[j - 1], on_ctx(i))

    def back_head(k):
        return ((4 - k // 2) % 4) * 2 + k % 2

    def b_piece(hh):
        return pl.ds(pl.multiple_of(hh * B_PIECE, 16), B_PIECE)

    HEAD_ORDER = (5, 3, 7, 4, 1, 2, 6)

    def b_ctx():
        part = chip[0, A_ROWS:, :].astype(f32)
        for j in range(1, 8):
            b1_copy[j].wait_recv()
            part = part + brecv[j - 1].astype(f32)
        bsum[...] = part.astype(bf16)
        for k in HEAD_ORDER:
            j = back_head(k)
            b2_copy[j] = send(
                bsum.at[b_piece(head_of(k))], b2recv.at[j - 1],
                b2_ssem.at[j - 1], b2_rsem.at[j - 1], on_head(k),
            )

    def a_ctx():
        part = asum[0].astype(f32)
        for j in range(1, 8):
            a2_copy[j].wait_recv()
            part = part + a2recv[j - 1].astype(f32)
        a3[...] = part.astype(bf16)
        for k in HEAD_ORDER:
            j = back_head(k)
            a3_copy[j] = send(a3, a3recv.at[j - 1], a3_ssem.at[j - 1], a3_rsem.at[j - 1], on_head(k))

    def b_head():
        part = bsum[b_piece(head), :].astype(f32)
        for j in range(1, 8):
            b2_copy[j].wait_recv()
            part = part + b2recv[j - 1].astype(f32)
        b3[...] = part.astype(bf16)
        for k in HEAD_ORDER:
            j = back_head(k)
            b3_copy[j] = send(b3, b3recv.at[j - 1], b3_ssem.at[j - 1], b3_rsem.at[j - 1], on_head(k))

    def finish():
        for j in range(1, 8):
            a3_copy[j].wait_recv()
        for dx in range(4):
            first = a3[...] if dx == 0 else a3recv[2 * dx - 1]
            both = first.astype(f32) + a3recv[2 * dx].astype(f32)
            out_t[piece(lax.rem(x + dx, 4)), :] = both.astype(bf16)
        for j in range(8):
            if j:
                b3_copy[j].wait_recv()
            rows = pl.ds(pl.multiple_of(A_ROWS + head_of(j) * B_PIECE, 16), B_PIECE)
            out_t[rows, :] = b3recv[j - 1] if j else b3[...]

    out_copy = []

    def row_outputs(n):
        if n < 2:
            left, wide, out, first = prob_b, LAT, at_v, n * 256
        else:
            left, wide, out, first = dscore, KD, qg_v, (n - 2) * 256
        size = min(256, wide - first)
        keys = jnp.concatenate([k_t[j, first : first + size, :] for j in range(2 * CHIPS)], axis=1)
        part = dot(left[...], keys, NT)
        if n >= 2:
            part = part * SCALE
        for h in range(HEADS):
            out[:, h * wide + first : h * wide + first + size] = part[h * TOK : (h + 1) * TOK].astype(bf16)
        if n == 1:
            out_copy.append(pltpu.make_async_copy(at_v, at_hbm, out_sem.at[0]))
            out_copy[-1].start()
        if n == 4:
            out_copy.append(pltpu.make_async_copy(qg_v, qg_hbm, out_sem.at[1]))
            out_copy[-1].start()

    groups = [B_ORDER[n : n + 2] for n in range(0, CHIPS, 2)]
    for i in groups[0]:
        weights(i)
    for n, group in enumerate(groups):
        if n + 1 < len(groups):
            for i in groups[n + 1]:
                weights(i)
        for i in group:
            key_grads(i)
        for i in group:
            to_core(i)
        if n >= 1:
            for i in groups[n - 1]:
                to_links(i)
    row_outputs(0)
    for i in groups[3]:
        to_links(i)
    sum_x(B_ORDER[0])
    sum_x(B_ORDER[1])
    sum_x(B_ORDER[2])
    sum_x(B_ORDER[3])
    row_outputs(1)
    row_outputs(2)
    sum_x(B_ORDER[4])
    sum_x(B_ORDER[5])
    sum_x(B_ORDER[6])
    sum_x(B_ORDER[7])
    b_ctx()
    row_outputs(3)
    a_ctx()
    b_head()
    row_outputs(4)
    finish()
    kg_copy = pltpu.make_async_copy(out_t, kg_hbm, in_sem.at[0])
    kg_copy.start()

    for group in (z_copy, y_copy, q_copy, x_copy, f_copy, c_copy, a1_copy, a2_copy, a3_copy, b1_copy, b2_copy, b3_copy):
        for copy in group.values():
            copy.wait_send()
    for copy in out_copy:
        copy.wait()
    kg_copy.wait()


def place(*refs):
    srcs, dsts, held, sems = refs[:3], refs[3:6], refs[6:9], refs[9]
    copies = []
    for n in range(3):
        rows = srcs[n].shape[0] // SPLIT
        for c in range(SPLIT):
            part = pl.ds(c * rows, rows)
            into = pltpu.make_async_copy(srcs[n].at[part], held[n].at[part], sems.at[0, n, c])
            out = pltpu.make_async_copy(held[n].at[part], dsts[n].at[part], sems.at[1, n, c])
            into.start()
            copies.append((into, out))
    for into, out in copies:
        into.wait()
        out.start()
    for into, out in copies:
        out.wait()


def local(queries, latent_keys, block_order, out_grad):
    f32, bf16 = jnp.float32, jnp.bfloat16
    vmem, dma = pltpu.VMEM, pltpu.SemaphoreType.DMA
    anywhere = pl.BlockSpec(memory_space=pl.ANY)
    scratch = [
        vmem((TOK, HEADS * KD), bf16), vmem((TOK, HEADS * LAT), bf16),
        vmem((ROWS, KD), bf16), vmem((ROWS, LAT), bf16), vmem((KD, ROWS), bf16), vmem((LAT, ROWS), bf16),
        vmem((2 * CHIPS, KD, TOK), bf16),
        vmem((ROWS, KEYS), f32), vmem((ROWS, KEYS), f32),
        vmem((ROWS, TOK), f32), vmem((ROWS, TOK), f32), vmem((ROWS, TOK), f32),
        vmem((ROWS, TOK), f32), vmem((ROWS, TOK), f32),
        vmem((ROWS, KEYS), bf16), vmem((ROWS, KEYS), bf16),
        vmem((CHIPS, KD, TOK), f32), vmem((CHIPS, KD, TOK), bf16), vmem((CHIPS, KD, TOK), bf16),
        vmem((CHIPS, KD, TOK), bf16),
        vmem((CHIPS, 3, A_PIECE, TOK), bf16), vmem((CHIPS, A_PIECE, TOK), bf16),
        vmem((7, A_PIECE, TOK), bf16), vmem((A_PIECE, TOK), bf16), vmem((7, A_PIECE, TOK), bf16),
        vmem((7, B_ROWS, TOK), bf16), vmem((B_ROWS, TOK), bf16), vmem((7, B_PIECE, TOK), bf16),
        vmem((B_PIECE, TOK), bf16), vmem((7, B_PIECE, TOK), bf16),
        vmem((KD, TOK), bf16),
        vmem((TOK, HEADS * LAT), bf16), vmem((TOK, HEADS * KD), bf16),
        dma((3,)), dma((2,)),
        dma((4, PARTS)), dma((4, PARTS)), dma((4, PARTS)), dma((4, PARTS)), dma((2,)), dma((2,)), dma((2, 3)), dma((2, 3)),
        dma((8,)), dma((8,)),
        dma((8,)), dma((8,)), dma((8, 3)), dma((8, 3)), dma((7,)), dma((7,)), dma((7,)), dma((7,)),
        dma((7,)), dma((7,)), dma((7,)), dma((7,)), dma((7,)), dma((7,)),
    ]
    attended, query_grad, key_grad = pl.pallas_call(
        kernel,
        out_shape=[
            jax.ShapeDtypeStruct((TOK, HEADS * LAT), bf16),
            jax.ShapeDtypeStruct((TOK, HEADS * KD), bf16),
            jax.ShapeDtypeStruct((KD, TOK), bf16),
        ],
        in_specs=[pl.BlockSpec(memory_space=pltpu.SMEM), anywhere, anywhere, anywhere],
        out_specs=[anywhere, anywhere, anywhere],
        scratch_shapes=scratch,
        compiler_params=pltpu.CompilerParams(
            collective_id=0, has_side_effects=True, vmem_limit_bytes=60 * 2**20
        ),
        cost_estimate=pl.CostEstimate(flops=14 * 10**9, bytes_accessed=5 * 10**6, transcendentals=4 * 10**6),
    )(block_order, queries, latent_keys.T, out_grad)
    results = (attended, query_grad, key_grad)
    attended, query_grad, key_grad = pl.pallas_call(
        place,
        out_shape=[jax.ShapeDtypeStruct(r.shape, r.dtype) for r in results],
        in_specs=[anywhere] * 3,
        out_specs=[anywhere] * 3,
        scratch_shapes=[vmem(r.shape, r.dtype) for r in results] + [dma((2, 3, SPLIT))],
    )(*results)
    return attended, query_grad, key_grad.T


def solution(mesh):
    return jax.shard_map(
        local,
        mesh=mesh,
        in_specs=(P("ctx", "head"), P("ctx", None), P(), P("ctx", "head")),
        out_specs=(P("ctx", "head"), P("ctx", "head"), P("ctx", None)),
        check_vma=False,
    )
```

```python
import functools

import jax
import jax.numpy as jnp
from jax import lax
from jax.experimental import pallas as pl
from jax.experimental.pallas import tpu as pltpu
from jax.sharding import PartitionSpec as P

HEADS = 8
TOK = 128
LAT = 512
KD = 576
ROWS = HEADS * TOK
CHIPS = 8
KEYS = CHIPS * 2 * TOK
SCALE = 192.0**-0.5
LOG2E = 1.4426950408889634
MASKED = -1.0e30
MESH = pl.DeviceIdType.MESH

PARTS = 4
PART = KD // PARTS
A_PIECE = 80
A_ROWS = 4 * A_PIECE
B_ROWS = KD - A_ROWS
B_PIECE = B_ROWS // 8

NN = (((1,), (0,)), ((), ()))
NT = (((1,), (1,)), ((), ()))

B_ORDER = (6, 5, 7, 2, 4, 1, 3, 0)


def back(i):
    return (i // 4) * 4 + (4 - i % 4) % 4


def dot(a, b, dims):
    return lax.dot_general(a, b, dims, preferred_element_type=jnp.float32)


def kernel(
    order_ref, q_hbm, k_hbm, g_hbm,
    at_v, qg_v, out_t,
    q_in, g_in, q_s, g_s, q_t, g_t, k_t,
    score, dprob, top, total, weighted, lse, delta, prob_b, dscore,
    mine, csend, crecv, chip, arecv, asum, a2recv, a3, a3recv,
    brecv, bsum, b2recv, b3, b3recv,
    in_sem,
    z_send, z_recv, y_send, y_recv, q_send, q_recv, x_send, x_recv, f_send, f_recv,
    c_ssem, c_rsem, a1_ssem, a1_rsem, a2_ssem, a2_rsem, a3_ssem, a3_rsem,
    b1_ssem, b1_rsem, b2_ssem, b2_rsem, b3_ssem, b3_rsem,
):
    f32, bf16 = jnp.float32, jnp.bfloat16
    ctx, head = lax.axis_index("ctx"), lax.axis_index("head")
    core = lax.rem(ctx, 2)
    z = lax.rem(ctx // 2, 4)
    y_lo = ctx // 8
    x, y_hi = head // 2, lax.rem(head, 2)

    def chip_of(i, other=0):
        yy = lax.rem(y_lo + i // 4, 2)
        zz = lax.rem(z + i % 4, 4)
        cc = lax.rem(core + other, 2)
        return (yy * 4 + zz) * 2 + cc

    def on_ctx(i):
        return (chip_of(i), head)

    def head_of(k):
        return lax.rem(x + k // 2, 4) * 2 + lax.rem(y_hi + k % 2, 2)

    def on_head(k):
        return (ctx, head_of(k))

    peer = (chip_of(0, 1), head)

    def y_neighbour(step):
        y = lax.rem(y_hi * 2 + y_lo + step, 4)
        return ((lax.rem(y, 2) * 4 + z) * 2 + core, x * 2 + y // 2)

    y_next = (y_neighbour(1), y_neighbour(3))

    load_k = pltpu.make_async_copy(k_hbm, k_t.at[0], in_sem.at[0])
    load_q = pltpu.make_async_copy(q_hbm, q_in, in_sem.at[1])
    load_g = pltpu.make_async_copy(g_hbm, g_in, in_sem.at[2])
    load_k.start()
    load_q.start()
    load_g.start()

    barrier = pltpu.get_barrier_semaphore()
    others = [peer, y_next[0], y_next[1]] + [on_ctx(i) for i in (1, 3, 2, 6)] + [on_head(k) for k in (2, 6, 4)]
    for other in others:
        pl.semaphore_signal(barrier, inc=1, device_id=other, device_id_type=MESH)

    def slot(i, u):
        return pl.ds((2 * i + u) * TOK, TOK)

    def keys_at(i, u=0):
        return k_t.at[2 * i + u]

    def send(src, dst, ssem, rsem, device):
        copy = pltpu.make_async_remote_copy(
            src_ref=src, dst_ref=dst, send_sem=ssem, recv_sem=rsem,
            device_id=device, device_id_type=MESH,
        )
        copy.start()
        return copy

    pl.semaphore_wait(barrier, len(others))

    def part_of(j, c):
        return k_t.at[j, pl.ds(c * PART, PART)]

    quarter = pl.ds(pl.multiple_of(x * PART, 16), PART)
    z_copy, y_copy, q_copy, x_copy, f_copy = {}, {}, {}, {}, {}

    def along_z(i, c):
        j = back(i)
        z_copy[j, c] = send(
            k_hbm.at[pl.ds(c * PART, PART)], part_of(2 * j, c), z_send.at[j, c], z_recv.at[j, c], on_ctx(i)
        )

    def across_y(i, c):
        src = part_of(2 * i, c) if i else k_hbm.at[pl.ds(c * PART, PART)]
        y_copy[4 + i, c] = send(src, part_of(2 * (4 + i), c), y_send.at[i, c], y_recv.at[i, c], y_next[c % 2])

    def fetch(i):
        q_copy[i] = send(
            k_hbm.at[quarter], k_t.at[2 * i, quarter], q_send.at[i // 4], q_recv.at[i // 4], on_ctx(i)
        )

    def along_x(i):
        q_copy[i].wait_recv()
        for dx in (2, 1, 3):
            n = 3 - dx
            x_copy[i, n] = send(
                k_t.at[2 * i, quarter], k_t.at[2 * i, quarter],
                x_send.at[i // 4, n], x_recv.at[i // 4, n], on_head(2 * dx),
            )

    def to_other(i):
        src = keys_at(i) if i else k_hbm
        f_copy[i] = send(src, keys_at(i, 1), f_send.at[i], f_recv.at[i], peer)

    def from_z(i, c):
        z_copy[i, c].wait_recv()
        across_y(i, c)

    def from_y(i):
        for c in range(PARTS):
            y_copy[i, c].wait_recv()
        to_other(i)

    def from_x(i):
        for n in range(3):
            x_copy[i, n].wait_recv()
        to_other(i)

    fetch(6)
    fetch(2)
    for c in range(PARTS):
        along_z(1, c)
        along_z(3, c)
        across_y(0, c)
    to_other(0)

    load_q.wait()
    load_g.wait()
    for h in range(HEADS):
        rows = pl.ds(h * TOK, TOK)
        qh = q_in[:, h * KD : (h + 1) * KD]
        q_s[rows, :] = qh
        q_t[:, rows] = (qh.astype(f32) * SCALE).astype(bf16).T
        gh = g_in[:, h * LAT : (h + 1) * LAT]
        g_s[rows, :] = gh
        g_t[:, rows] = gh.T

    top[...] = jnp.full((ROWS, TOK), MASKED, f32)
    total[...] = jnp.zeros((ROWS, TOK), f32)
    weighted[...] = jnp.zeros((ROWS, TOK), f32)
    ahead = lax.broadcasted_iota(jnp.int32, (TOK, TOK), 1) - lax.broadcasted_iota(jnp.int32, (TOK, TOK), 0)
    my_block = order_ref[ctx]

    def scores(first, second):
        pair = (first, second)
        keys = jnp.concatenate([k_t[2 * i + u] for i, u in pair], axis=1)
        visible = [ahead <= (my_block - order_ref[chip_of(i, u)]) * TOK for i, u in pair]
        for h in range(HEADS):
            rows = pl.ds(h * TOK, TOK)
            sc = dot(q_s[rows, :], keys, NN) * (SCALE * LOG2E)
            dp = dot(g_s[rows, :], keys[:LAT], NN)
            s0 = jnp.where(visible[0], sc[:, :TOK], MASKED)
            s1 = jnp.where(visible[1], sc[:, TOK:], MASKED)
            score[rows, slot(*first)] = s0
            score[rows, slot(*second)] = s1
            dprob[rows, slot(*first)] = dp[:, :TOK]
            dprob[rows, slot(*second)] = dp[:, TOK:]
            m0 = top[rows, :]
            m1 = jnp.maximum(m0, jnp.maximum(s0, s1))
            shrink = jnp.exp2(m0 - m1)
            e0, e1 = jnp.exp2(s0 - m1), jnp.exp2(s1 - m1)
            top[rows, :] = m1
            total[rows, :] = total[rows, :] * shrink + (e0 + e1)
            weighted[rows, :] = weighted[rows, :] * shrink + (e0 * dp[:, :TOK] + e1 * dp[:, TOK:])

    load_k.wait()
    f_copy[0].wait_recv()
    scores((0, 0), (0, 1))
    along_x(2)
    along_x(6)
    for c in range(PARTS):
        from_z(1, c)
        from_z(3, c)
    to_other(1)
    to_other(3)
    scores((1, 0), (3, 0))
    from_y(4)
    f_copy[1].wait_recv()
    f_copy[3].wait_recv()
    scores((1, 1), (3, 1))
    f_copy[4].wait_recv()
    scores((4, 0), (4, 1))
    from_x(2)
    from_x(6)
    scores((2, 0), (6, 0))
    from_y(5)
    from_y(7)
    scores((5, 0), (7, 0))
    f_copy[2].wait_recv()
    f_copy[6].wait_recv()
    scores((2, 1), (6, 1))
    f_copy[5].wait_recv()
    f_copy[7].wait_recv()
    scores((5, 1), (7, 1))

    for h in range(HEADS):
        rows = pl.ds(h * TOK, TOK)
        lane_top = top[rows, :]
        row_top = jnp.max(lane_top, axis=1, keepdims=True)
        weight = jnp.exp2(lane_top - row_top)
        row_total = jnp.sum(total[rows, :] * weight, axis=1, keepdims=True)
        row_weighted = jnp.sum(weighted[rows, :] * weight, axis=1, keepdims=True)
        lse[rows, :] = jnp.broadcast_to(row_top + jnp.log2(row_total), (TOK, TOK))
        delta[rows, :] = jnp.broadcast_to(row_weighted / row_total, (TOK, TOK))

    def weights(i):
        for u in range(2):
            cols = slot(i, u)
            p = jnp.exp2(score[:, cols] - lse[...])
            prob_b[:, cols] = p.astype(bf16)
            dscore[:, cols] = (p * (dprob[:, cols] - delta[...])).astype(bf16)

    c_copy, a1_copy, a2_copy, a3_copy = {}, {}, {}, {}
    b1_copy, b2_copy, b3_copy = {}, {}, {}

    def key_grads(i):
        cols = pl.ds(2 * i * TOK, 2 * TOK)
        from_scores = dot(q_t[...], dscore[:, cols], NN)
        from_values = dot(g_t[...], prob_b[:, cols], NN)
        low = from_scores[:LAT] + from_values
        high = from_scores[LAT:]
        mine[i, :LAT, :] = low[:, :TOK]
        mine[i, LAT:, :] = high[:, :TOK]
        csend[i, :LAT, :] = low[:, TOK:].astype(bf16)
        csend[i, LAT:, :] = high[:, TOK:].astype(bf16)

    def to_core(i):
        c_copy[i] = send(csend.at[i], crecv.at[i], c_ssem.at[i], c_rsem.at[i], peer)

    def piece(xx):
        return pl.ds(pl.multiple_of(xx * A_PIECE, 16), A_PIECE)

    def to_links(i):
        c_copy[i].wait_recv()
        chip[i] = (mine[i] + crecv[i].astype(f32)).astype(bf16)
        for dx in (2, 1, 3):
            a1_copy[i, 4 - dx] = send(
                chip.at[i, piece(lax.rem(x + dx, 4))], arecv.at[i, 4 - dx - 1],
                a1_ssem.at[i, 4 - dx - 1], a1_rsem.at[i, 4 - dx - 1], on_head(2 * dx),
            )
        if i:
            j = back(i)
            b1_copy[j] = send(
                chip.at[i, pl.ds(A_ROWS, B_ROWS)], brecv.at[j - 1],
                b1_ssem.at[j - 1], b1_rsem.at[j - 1], on_ctx(i),
            )

    def sum_x(i):
        for dx in (1, 2, 3):
            a1_copy[i, dx].wait_recv()
        part = chip[i, piece(x), :].astype(f32)
        for n in range(3):
            part = part + arecv[i, n].astype(f32)
        asum[i] = part.astype(bf16)
        if i:
            j = back(i)
            a2_copy[j] = send(asum.at[i], a2recv.at[j - 1], a2_ssem.at[j - 1], a2_rsem.at[j - 1], on_ctx(i))

    def back_head(k):
        return ((4 - k // 2) % 4) * 2 + k % 2

    def b_piece(hh):
        return pl.ds(pl.multiple_of(hh * B_PIECE, 16), B_PIECE)

    HEAD_ORDER = (5, 3, 7, 4, 1, 2, 6)

    def b_ctx():
        part = chip[0, A_ROWS:, :].astype(f32)
        for j in range(1, 8):
            b1_copy[j].wait_recv()
            part = part + brecv[j - 1].astype(f32)
        bsum[...] = part.astype(bf16)
        for k in HEAD_ORDER:
            j = back_head(k)
            b2_copy[j] = send(
                bsum.at[b_piece(head_of(k))], b2recv.at[j - 1],
                b2_ssem.at[j - 1], b2_rsem.at[j - 1], on_head(k),
            )

    def a_ctx():
        part = asum[0].astype(f32)
        for j in range(1, 8):
            a2_copy[j].wait_recv()
            part = part + a2recv[j - 1].astype(f32)
        a3[...] = part.astype(bf16)
        for k in HEAD_ORDER:
            j = back_head(k)
            a3_copy[j] = send(a3, a3recv.at[j - 1], a3_ssem.at[j - 1], a3_rsem.at[j - 1], on_head(k))

    def b_head():
        part = bsum[b_piece(head), :].astype(f32)
        for j in range(1, 8):
            b2_copy[j].wait_recv()
            part = part + b2recv[j - 1].astype(f32)
        b3[...] = part.astype(bf16)
        for k in HEAD_ORDER:
            j = back_head(k)
            b3_copy[j] = send(b3, b3recv.at[j - 1], b3_ssem.at[j - 1], b3_rsem.at[j - 1], on_head(k))

    def finish():
        for j in range(1, 8):
            a3_copy[j].wait_recv()
        for dx in range(4):
            first = a3[...] if dx == 0 else a3recv[2 * dx - 1]
            both = first.astype(f32) + a3recv[2 * dx].astype(f32)
            out_t[piece(lax.rem(x + dx, 4)), :] = both.astype(bf16)
        for j in range(8):
            if j:
                b3_copy[j].wait_recv()
            rows = pl.ds(pl.multiple_of(A_ROWS + head_of(j) * B_PIECE, 16), B_PIECE)
            out_t[rows, :] = b3recv[j - 1] if j else b3[...]

    def row_outputs(n):
        if n < 2:
            left, wide, out, first = prob_b, LAT, at_v, n * 256
        else:
            left, wide, out, first = dscore, KD, qg_v, (n - 2) * 256
        size = min(256, wide - first)
        keys = jnp.concatenate([k_t[j, first : first + size, :] for j in range(2 * CHIPS)], axis=1)
        part = dot(left[...], keys, NT)
        if n >= 2:
            part = part * SCALE
        for h in range(HEADS):
            out[:, h * wide + first : h * wide + first + size] = part[h * TOK : (h + 1) * TOK].astype(bf16)

    groups = [B_ORDER[n : n + 2] for n in range(0, CHIPS, 2)]
    for i in groups[0]:
        weights(i)
    for n, group in enumerate(groups):
        if n + 1 < len(groups):
            for i in groups[n + 1]:
                weights(i)
        for i in group:
            key_grads(i)
        for i in group:
            to_core(i)
        if n >= 1:
            for i in groups[n - 1]:
                to_links(i)
    row_outputs(0)
    for i in groups[3]:
        to_links(i)
    sum_x(B_ORDER[0])
    sum_x(B_ORDER[1])
    sum_x(B_ORDER[2])
    sum_x(B_ORDER[3])
    row_outputs(1)
    row_outputs(2)
    sum_x(B_ORDER[4])
    sum_x(B_ORDER[5])
    sum_x(B_ORDER[6])
    sum_x(B_ORDER[7])
    b_ctx()
    row_outputs(3)
    a_ctx()
    b_head()
    row_outputs(4)
    finish()
    for group in (z_copy, y_copy, q_copy, x_copy, f_copy, c_copy, a1_copy, a2_copy, a3_copy, b1_copy, b2_copy, b3_copy):
        for copy in group.values():
            copy.wait_send()


def local(queries, latent_keys, block_order, out_grad):
    f32, bf16 = jnp.float32, jnp.bfloat16
    vmem, dma = pltpu.VMEM, pltpu.SemaphoreType.DMA
    anywhere = pl.BlockSpec(memory_space=pl.ANY)
    scratch = [
        vmem((TOK, HEADS * KD), bf16), vmem((TOK, HEADS * LAT), bf16),
        vmem((ROWS, KD), bf16), vmem((ROWS, LAT), bf16), vmem((KD, ROWS), bf16), vmem((LAT, ROWS), bf16),
        vmem((2 * CHIPS, KD, TOK), bf16),
        vmem((ROWS, KEYS), f32), vmem((ROWS, KEYS), f32),
        vmem((ROWS, TOK), f32), vmem((ROWS, TOK), f32), vmem((ROWS, TOK), f32),
        vmem((ROWS, TOK), f32), vmem((ROWS, TOK), f32),
        vmem((ROWS, KEYS), bf16), vmem((ROWS, KEYS), bf16),
        vmem((CHIPS, KD, TOK), f32), vmem((CHIPS, KD, TOK), bf16), vmem((CHIPS, KD, TOK), bf16),
        vmem((CHIPS, KD, TOK), bf16),
        vmem((CHIPS, 3, A_PIECE, TOK), bf16), vmem((CHIPS, A_PIECE, TOK), bf16),
        vmem((7, A_PIECE, TOK), bf16), vmem((A_PIECE, TOK), bf16), vmem((7, A_PIECE, TOK), bf16),
        vmem((7, B_ROWS, TOK), bf16), vmem((B_ROWS, TOK), bf16), vmem((7, B_PIECE, TOK), bf16),
        vmem((B_PIECE, TOK), bf16), vmem((7, B_PIECE, TOK), bf16),
        dma((3,)),
        dma((4, PARTS)), dma((4, PARTS)), dma((4, PARTS)), dma((4, PARTS)), dma((2,)), dma((2,)), dma((2, 3)), dma((2, 3)),
        dma((8,)), dma((8,)),
        dma((8,)), dma((8,)), dma((8, 3)), dma((8, 3)), dma((7,)), dma((7,)), dma((7,)), dma((7,)),
        dma((7,)), dma((7,)), dma((7,)), dma((7,)), dma((7,)), dma((7,)),
    ]
    attended, query_grad, key_grad = pl.pallas_call(
        kernel,
        out_shape=[
            vmem((TOK, HEADS * LAT), bf16), vmem((TOK, HEADS * KD), bf16), vmem((KD, TOK), bf16),
        ],
        in_specs=[pl.BlockSpec(memory_space=pltpu.SMEM), anywhere, anywhere, anywhere],
        out_specs=[pl.BlockSpec(memory_space=pltpu.VMEM)] * 3,
        scratch_shapes=scratch,
        compiler_params=pltpu.CompilerParams(
            collective_id=0, has_side_effects=True, vmem_limit_bytes=60 * 2**20
        ),
        cost_estimate=pl.CostEstimate(flops=14 * 10**9, bytes_accessed=5 * 10**6, transcendentals=4 * 10**6),
    )(block_order, queries, latent_keys.T, out_grad)
    return attended, query_grad, key_grad.T


def solution(mesh):
    return jax.shard_map(
        local,
        mesh=mesh,
        in_specs=(P("ctx", "head"), P("ctx", None), P(), P("ctx", "head")),
        out_specs=(P("ctx", "head"), P("ctx", "head"), P("ctx", None)),
        check_vma=False,
    )
```

```python
import functools

import jax
import jax.numpy as jnp
from jax import lax
from jax.experimental import pallas as pl
from jax.experimental.pallas import tpu as pltpu
from jax.sharding import PartitionSpec as P

HEADS = 8
TOK = 128
LAT = 512
KD = 576
ROWS = HEADS * TOK
CHIPS = 8
KEYS = CHIPS * 2 * TOK
SCALE = 192.0**-0.5
LOG2E = 1.4426950408889634
MASKED = -1.0e30
MESH = pl.DeviceIdType.MESH

PARTS = 4
PART = KD // PARTS
A_PIECE = 80
A_ROWS = 4 * A_PIECE
B_ROWS = KD - A_ROWS
B_PIECE = B_ROWS // 8

NN = (((1,), (0,)), ((), ()))
NT = (((1,), (1,)), ((), ()))

B_ORDER = (6, 5, 7, 2, 4, 1, 3, 0)


def back(i):
    return (i // 4) * 4 + (4 - i % 4) % 4


def dot(a, b, dims):
    return lax.dot_general(a, b, dims, preferred_element_type=jnp.float32)


def kernel(
    order_ref, q_hbm, k_hbm, g_hbm,
    at_v, qg_v, out_t,
    q_in, g_in, q_s, g_s, q_t, g_t, k_t,
    score, dprob, top, total, weighted, lse, delta, prob_b, dscore,
    mine, csend, crecv, chip, arecv, asum, a2recv, a3, a3recv,
    brecv, bsum, b2recv, b3, b3recv,
    in_sem,
    z_send, z_recv, y_send, y_recv, q_send, q_recv, x_send, x_recv, f_send, f_recv,
    c_ssem, c_rsem, a1_ssem, a1_rsem, a2_ssem, a2_rsem, a3_ssem, a3_rsem,
    b1_ssem, b1_rsem, b2_ssem, b2_rsem, b3_ssem, b3_rsem,
):
    f32, bf16 = jnp.float32, jnp.bfloat16
    ctx, head = lax.axis_index("ctx"), lax.axis_index("head")
    core = lax.rem(ctx, 2)
    z = lax.rem(ctx // 2, 4)
    y_lo = ctx // 8
    x, y_hi = head // 2, lax.rem(head, 2)

    def chip_of(i, other=0):
        yy = lax.rem(y_lo + i // 4, 2)
        zz = lax.rem(z + i % 4, 4)
        cc = lax.rem(core + other, 2)
        return (yy * 4 + zz) * 2 + cc

    def on_ctx(i):
        return (chip_of(i), head)

    def head_of(k):
        return lax.rem(x + k // 2, 4) * 2 + lax.rem(y_hi + k % 2, 2)

    def on_head(k):
        return (ctx, head_of(k))

    peer = (chip_of(0, 1), head)

    def y_neighbour(step):
        y = lax.rem(y_hi * 2 + y_lo + step, 4)
        return ((lax.rem(y, 2) * 4 + z) * 2 + core, x * 2 + y // 2)

    y_next = (y_neighbour(1), y_neighbour(3))

    load_k = pltpu.make_async_copy(k_hbm, k_t.at[0], in_sem.at[0])
    load_q = pltpu.make_async_copy(q_hbm, q_in, in_sem.at[1])
    load_g = pltpu.make_async_copy(g_hbm, g_in, in_sem.at[2])
    load_k.start()
    load_q.start()
    load_g.start()

    barrier = pltpu.get_barrier_semaphore()
    others = [peer, y_next[0], y_next[1]] + [on_ctx(i) for i in (1, 3, 2, 6)] + [on_head(k) for k in (2, 6, 4)]
    for other in others:
        pl.semaphore_signal(barrier, inc=1, device_id=other, device_id_type=MESH)

    def slot(i, u):
        return pl.ds((2 * i + u) * TOK, TOK)

    def keys_at(i, u=0):
        return k_t.at[2 * i + u]

    def send(src, dst, ssem, rsem, device):
        copy = pltpu.make_async_remote_copy(
            src_ref=src, dst_ref=dst, send_sem=ssem, recv_sem=rsem,
            device_id=device, device_id_type=MESH,
        )
        copy.start()
        return copy

    pl.semaphore_wait(barrier, len(others))

    def part_of(j, c):
        return k_t.at[j, pl.ds(c * PART, PART)]

    quarter = pl.ds(pl.multiple_of(x * PART, 16), PART)
    z_copy, y_copy, q_copy, x_copy, f_copy = {}, {}, {}, {}, {}

    def along_z(i, c):
        j = back(i)
        z_copy[j, c] = send(
            k_hbm.at[pl.ds(c * PART, PART)], part_of(2 * j, c), z_send.at[j, c], z_recv.at[j, c], on_ctx(i)
        )

    def across_y(i, c):
        src = part_of(2 * i, c) if i else k_hbm.at[pl.ds(c * PART, PART)]
        y_copy[4 + i, c] = send(src, part_of(2 * (4 + i), c), y_send.at[i, c], y_recv.at[i, c], y_next[c % 2])

    def fetch(i):
        q_copy[i] = send(
            k_hbm.at[quarter], k_t.at[2 * i, quarter], q_send.at[i // 4], q_recv.at[i // 4], on_ctx(i)
        )

    def along_x(i):
        q_copy[i].wait_recv()
        for dx in (2, 1, 3):
            n = 3 - dx
            x_copy[i, n] = send(
                k_t.at[2 * i, quarter], k_t.at[2 * i, quarter],
                x_send.at[i // 4, n], x_recv.at[i // 4, n], on_head(2 * dx),
            )

    def to_other(i):
        src = keys_at(i) if i else k_hbm
        f_copy[i] = send(src, keys_at(i, 1), f_send.at[i], f_recv.at[i], peer)

    def from_z(i, c):
        z_copy[i, c].wait_recv()
        across_y(i, c)

    def from_y(i):
        for c in range(PARTS):
            y_copy[i, c].wait_recv()
        to_other(i)

    def from_x(i):
        for n in range(3):
            x_copy[i, n].wait_recv()
        to_other(i)

    fetch(6)
    fetch(2)
    for c in range(PARTS):
        along_z(1, c)
        along_z(3, c)
        across_y(0, c)
    to_other(0)

    load_q.wait()
    load_g.wait()
    for h in range(HEADS):
        rows = pl.ds(h * TOK, TOK)
        qh = q_in[:, h * KD : (h + 1) * KD]
        q_s[rows, :] = qh
        q_t[:, rows] = (qh.astype(f32) * SCALE).astype(bf16).T
        gh = g_in[:, h * LAT : (h + 1) * LAT]
        g_s[rows, :] = gh
        g_t[:, rows] = gh.T

    top[...] = jnp.full((ROWS, TOK), MASKED, f32)
    total[...] = jnp.zeros((ROWS, TOK), f32)
    weighted[...] = jnp.zeros((ROWS, TOK), f32)
    ahead = lax.broadcasted_iota(jnp.int32, (TOK, TOK), 1) - lax.broadcasted_iota(jnp.int32, (TOK, TOK), 0)
    my_block = order_ref[ctx]

    def scores(first, second):
        pair = (first, second)
        keys = jnp.concatenate([k_t[2 * i + u] for i, u in pair], axis=1)
        visible = [ahead <= (my_block - order_ref[chip_of(i, u)]) * TOK for i, u in pair]
        for h in range(HEADS):
            rows = pl.ds(h * TOK, TOK)
            sc = dot(q_s[rows, :], keys, NN) * (SCALE * LOG2E)
            dp = dot(g_s[rows, :], keys[:LAT], NN)
            s0 = jnp.where(visible[0], sc[:, :TOK], MASKED)
            s1 = jnp.where(visible[1], sc[:, TOK:], MASKED)
            score[rows, slot(*first)] = s0
            score[rows, slot(*second)] = s1
            dprob[rows, slot(*first)] = dp[:, :TOK]
            dprob[rows, slot(*second)] = dp[:, TOK:]
            m0 = top[rows, :]
            m1 = jnp.maximum(m0, jnp.maximum(s0, s1))
            shrink = jnp.exp2(m0 - m1)
            e0, e1 = jnp.exp2(s0 - m1), jnp.exp2(s1 - m1)
            top[rows, :] = m1
            total[rows, :] = total[rows, :] * shrink + (e0 + e1)
            weighted[rows, :] = weighted[rows, :] * shrink + (e0 * dp[:, :TOK] + e1 * dp[:, TOK:])

    load_k.wait()
    f_copy[0].wait_recv()
    scores((0, 0), (0, 1))
    along_x(2)
    along_x(6)
    for c in range(PARTS):
        from_z(1, c)
        from_z(3, c)
    to_other(1)
    to_other(3)
    scores((1, 0), (3, 0))
    from_y(4)
    f_copy[1].wait_recv()
    f_copy[3].wait_recv()
    scores((1, 1), (3, 1))
    f_copy[4].wait_recv()
    scores((4, 0), (4, 1))
    from_x(2)
    from_x(6)
    scores((2, 0), (6, 0))
    from_y(5)
    from_y(7)
    scores((5, 0), (7, 0))
    f_copy[2].wait_recv()
    f_copy[6].wait_recv()
    scores((2, 1), (6, 1))
    f_copy[5].wait_recv()
    f_copy[7].wait_recv()
    scores((5, 1), (7, 1))

    for h in range(HEADS):
        rows = pl.ds(h * TOK, TOK)
        lane_top = top[rows, :]
        row_top = jnp.max(lane_top, axis=1, keepdims=True)
        weight = jnp.exp2(lane_top - row_top)
        row_total = jnp.sum(total[rows, :] * weight, axis=1, keepdims=True)
        row_weighted = jnp.sum(weighted[rows, :] * weight, axis=1, keepdims=True)
        lse[rows, :] = jnp.broadcast_to(row_top + jnp.log2(row_total), (TOK, TOK))
        delta[rows, :] = jnp.broadcast_to(row_weighted / row_total, (TOK, TOK))

    def weights(i):
        for u in range(2):
            cols = slot(i, u)
            p = jnp.exp2(score[:, cols] - lse[...])
            prob_b[:, cols] = p.astype(bf16)
            dscore[:, cols] = (p * (dprob[:, cols] - delta[...])).astype(bf16)

    c_copy, a1_copy, a2_copy, a3_copy = {}, {}, {}, {}
    b1_copy, b2_copy, b3_copy = {}, {}, {}

    def key_grads(i):
        cols = pl.ds(2 * i * TOK, 2 * TOK)
        from_scores = dot(q_t[...], dscore[:, cols], NN)
        from_values = dot(g_t[...], prob_b[:, cols], NN)
        low = from_scores[:LAT] + from_values
        high = from_scores[LAT:]
        mine[i, :LAT, :] = low[:, :TOK]
        mine[i, LAT:, :] = high[:, :TOK]
        csend[i, :LAT, :] = low[:, TOK:].astype(bf16)
        csend[i, LAT:, :] = high[:, TOK:].astype(bf16)

    def to_core(i):
        c_copy[i] = send(csend.at[i], crecv.at[i], c_ssem.at[i], c_rsem.at[i], peer)

    def piece(xx):
        return pl.ds(pl.multiple_of(xx * A_PIECE, 16), A_PIECE)

    def to_links(i):
        c_copy[i].wait_recv()
        chip[i] = (mine[i] + crecv[i].astype(f32)).astype(bf16)
        for dx in (2, 1, 3):
            a1_copy[i, 4 - dx] = send(
                chip.at[i, piece(lax.rem(x + dx, 4))], arecv.at[i, 4 - dx - 1],
                a1_ssem.at[i, 4 - dx - 1], a1_rsem.at[i, 4 - dx - 1], on_head(2 * dx),
            )
        if i:
            j = back(i)
            b1_copy[j] = send(
                chip.at[i, pl.ds(A_ROWS, B_ROWS)], brecv.at[j - 1],
                b1_ssem.at[j - 1], b1_rsem.at[j - 1], on_ctx(i),
            )

    def sum_x(i):
        for dx in (1, 2, 3):
            a1_copy[i, dx].wait_recv()
        part = chip[i, piece(x), :].astype(f32)
        for n in range(3):
            part = part + arecv[i, n].astype(f32)
        asum[i] = part.astype(bf16)
        if i:
            j = back(i)
            a2_copy[j] = send(asum.at[i], a2recv.at[j - 1], a2_ssem.at[j - 1], a2_rsem.at[j - 1], on_ctx(i))

    def back_head(k):
        return ((4 - k // 2) % 4) * 2 + k % 2

    def b_piece(hh):
        return pl.ds(pl.multiple_of(hh * B_PIECE, 16), B_PIECE)

    HEAD_ORDER = (5, 3, 7, 4, 1, 2, 6)

    def b_ctx():
        part = chip[0, A_ROWS:, :].astype(f32)
        for j in range(1, 8):
            b1_copy[j].wait_recv()
            part = part + brecv[j - 1].astype(f32)
        bsum[...] = part.astype(bf16)
        for k in HEAD_ORDER:
            j = back_head(k)
            b2_copy[j] = send(
                bsum.at[b_piece(head_of(k))], b2recv.at[j - 1],
                b2_ssem.at[j - 1], b2_rsem.at[j - 1], on_head(k),
            )

    def a_ctx():
        part = asum[0].astype(f32)
        for j in range(1, 8):
            a2_copy[j].wait_recv()
            part = part + a2recv[j - 1].astype(f32)
        a3[...] = part.astype(bf16)
        for k in HEAD_ORDER:
            j = back_head(k)
            a3_copy[j] = send(a3, a3recv.at[j - 1], a3_ssem.at[j - 1], a3_rsem.at[j - 1], on_head(k))

    def b_head():
        part = bsum[b_piece(head), :].astype(f32)
        for j in range(1, 8):
            b2_copy[j].wait_recv()
            part = part + b2recv[j - 1].astype(f32)
        b3[...] = part.astype(bf16)
        for k in HEAD_ORDER:
            j = back_head(k)
            b3_copy[j] = send(b3, b3recv.at[j - 1], b3_ssem.at[j - 1], b3_rsem.at[j - 1], on_head(k))

    def finish():
        for j in range(1, 8):
            a3_copy[j].wait_recv()
        for dx in range(4):
            first = a3[...] if dx == 0 else a3recv[2 * dx - 1]
            both = first.astype(f32) + a3recv[2 * dx].astype(f32)
            out_t[piece(lax.rem(x + dx, 4)), :] = both.astype(bf16)
        for j in range(8):
            if j:
                b3_copy[j].wait_recv()
            rows = pl.ds(pl.multiple_of(A_ROWS + head_of(j) * B_PIECE, 16), B_PIECE)
            out_t[rows, :] = b3recv[j - 1] if j else b3[...]

    def row_outputs(n):
        if n < 2:
            left, wide, out, first = prob_b, LAT, at_v, n * 256
        else:
            left, wide, out, first = dscore, KD, qg_v, (n - 2) * 256
        size = min(256, wide - first)
        keys = jnp.concatenate([k_t[j, first : first + size, :] for j in range(2 * CHIPS)], axis=1)
        part = dot(left[...], keys, NT)
        if n >= 2:
            part = part * SCALE
        for h in range(HEADS):
            out[:, h * wide + first : h * wide + first + size] = part[h * TOK : (h + 1) * TOK].astype(bf16)

    groups = [B_ORDER[n : n + 2] for n in range(0, CHIPS, 2)]
    for i in groups[0]:
        weights(i)
    for n, group in enumerate(groups):
        if n + 1 < len(groups):
            for i in groups[n + 1]:
                weights(i)
        for i in group:
            key_grads(i)
        for i in group:
            to_core(i)
        if n >= 1:
            for i in groups[n - 1]:
                to_links(i)
    row_outputs(0)
    for i in groups[3]:
        to_links(i)
    for n in range(0, 4):
        sum_x(B_ORDER[n])
    row_outputs(1)
    for n in range(4, 8):
        sum_x(B_ORDER[n])
    b_ctx()
    row_outputs(2)
    a_ctx()
    b_head()
    row_outputs(3)
    row_outputs(4)
    finish()
    for group in (z_copy, y_copy, q_copy, x_copy, f_copy, c_copy, a1_copy, a2_copy, a3_copy, b1_copy, b2_copy, b3_copy):
        for copy in group.values():
            copy.wait_send()


def local(queries, latent_keys, block_order, out_grad):
    f32, bf16 = jnp.float32, jnp.bfloat16
    vmem, dma = pltpu.VMEM, pltpu.SemaphoreType.DMA
    anywhere = pl.BlockSpec(memory_space=pl.ANY)
    scratch = [
        vmem((TOK, HEADS * KD), bf16), vmem((TOK, HEADS * LAT), bf16),
        vmem((ROWS, KD), bf16), vmem((ROWS, LAT), bf16), vmem((KD, ROWS), bf16), vmem((LAT, ROWS), bf16),
        vmem((2 * CHIPS, KD, TOK), bf16),
        vmem((ROWS, KEYS), f32), vmem((ROWS, KEYS), f32),
        vmem((ROWS, TOK), f32), vmem((ROWS, TOK), f32), vmem((ROWS, TOK), f32),
        vmem((ROWS, TOK), f32), vmem((ROWS, TOK), f32),
        vmem((ROWS, KEYS), bf16), vmem((ROWS, KEYS), bf16),
        vmem((CHIPS, KD, TOK), f32), vmem((CHIPS, KD, TOK), bf16), vmem((CHIPS, KD, TOK), bf16),
        vmem((CHIPS, KD, TOK), bf16),
        vmem((CHIPS, 3, A_PIECE, TOK), bf16), vmem((CHIPS, A_PIECE, TOK), bf16),
        vmem((7, A_PIECE, TOK), bf16), vmem((A_PIECE, TOK), bf16), vmem((7, A_PIECE, TOK), bf16),
        vmem((7, B_ROWS, TOK), bf16), vmem((B_ROWS, TOK), bf16), vmem((7, B_PIECE, TOK), bf16),
        vmem((B_PIECE, TOK), bf16), vmem((7, B_PIECE, TOK), bf16),
        dma((3,)),
        dma((4, PARTS)), dma((4, PARTS)), dma((4, PARTS)), dma((4, PARTS)), dma((2,)), dma((2,)), dma((2, 3)), dma((2, 3)),
        dma((8,)), dma((8,)),
        dma((8,)), dma((8,)), dma((8, 3)), dma((8, 3)), dma((7,)), dma((7,)), dma((7,)), dma((7,)),
        dma((7,)), dma((7,)), dma((7,)), dma((7,)), dma((7,)), dma((7,)),
    ]
    attended, query_grad, key_grad = pl.pallas_call(
        kernel,
        out_shape=[
            vmem((TOK, HEADS * LAT), bf16), vmem((TOK, HEADS * KD), bf16), vmem((KD, TOK), bf16),
        ],
        in_specs=[pl.BlockSpec(memory_space=pltpu.SMEM), anywhere, anywhere, anywhere],
        out_specs=[pl.BlockSpec(memory_space=pltpu.VMEM)] * 3,
        scratch_shapes=scratch,
        compiler_params=pltpu.CompilerParams(
            collective_id=0, has_side_effects=True, vmem_limit_bytes=60 * 2**20
        ),
        cost_estimate=pl.CostEstimate(flops=14 * 10**9, bytes_accessed=5 * 10**6, transcendentals=4 * 10**6),
    )(block_order, queries, latent_keys.T, out_grad)
    return attended, query_grad, key_grad.T


def solution(mesh):
    return jax.shard_map(
        local,
        mesh=mesh,
        in_specs=(P("ctx", "head"), P("ctx", None), P(), P("ctx", "head")),
        out_specs=(P("ctx", "head"), P("ctx", "head"), P("ctx", None)),
        check_vma=False,
    )
```
